768 devices in a mesh: xy: 32 (over x, y), gz: 24 (over z, core).
Axes of the slice: x: 4, y: 8, z: 12, core: 2. Of those that a mesh axis runs over, the one named last changes fastest.
Arguments:
- velocity: float32 [3, 96, 1024, 1024], P(None, 'gz', 'xy'), may hold values from -6 to 6
- magnetic: float32 [3, 48, 512, 512], P(None, 'gz', 'xy'), may hold values from -6 to 6
- slot_block_table: int32 [1024], P('xy'), may hold values from 0 to 1023, as said below
Outputs:
- updated_fine_velocity: float32 [3, 96, 1024, 1024], P(None, 'gz', 'xy')
- magnetic_next: float32 [3, 48, 512, 512], P(None, 'gz', 'xy')
The draws below stay inside these ranges and needn't reach their ends.
Inputs may be any that keep to these rules, and one draw needn't show every extreme that they name: `slot_block_table`: each block number appears in one slot; the 32 slots of one device along xy hold exactly 1 block of every block row.
All inputs are finite; a program needn't handle non-finite values.
Results may differ from the reference program's by a relative error of at most 0.00005.
Values sent between devices are 32-bit elements; how exact they have to be, the bound alone decides.
A program may use at most 64 MiB of HBM per device.

```python
import jax
import jax.numpy as jnp

BLOCK_EDGE = 32
BCOLS = 32
BROWS = 32
FBLOCKS = 1024
NZF = 96
NZC = 48
NYC = 512
NXC = 512


def draw_slot_block_table(key, part):
    share = BCOLS // BROWS
    row_keys = jax.random.split(jax.random.fold_in(key, 11), BROWS)
    perms = jax.vmap(lambda k: jax.random.permutation(k, BCOLS))(row_keys)
    holders = perms.reshape(BROWS, BROWS, share).transpose(1, 0, 2)
    rowbase = (jnp.arange(BROWS, dtype=jnp.int32) * BCOLS).reshape(1, BROWS, 1)
    listed = (holders.astype(jnp.int32) + rowbase).reshape(BROWS, BCOLS)
    slot_keys = jax.random.split(jax.random.fold_in(key, 23), BROWS)
    slots = jax.vmap(lambda k: jax.random.permutation(k, BCOLS))(slot_keys).astype(jnp.int32)
    return jnp.take_along_axis(listed, slots, axis=1).reshape(BROWS * BCOLS).astype(jnp.int32)


def block_scale(rng, dims, cuts, low, top_value):
    gain, own = 1.0, jax.random.fold_in(rng, 6)
    for dim, shards_of in cuts:
        heights = jnp.exp(jax.random.uniform(jax.random.fold_in(own, dim), (shards_of,), jnp.float32, low / len(cuts), top_value / len(cuts)))
        gain = gain * jnp.repeat(heights, dims[dim] // shards_of).reshape([-1 if axis == dim else 1 for axis in range(len(dims))])
    return gain


def scatter_about(rng, shape, scale, reach, cuts=(), held_as=jnp.bfloat16):
    loudness = block_scale(rng, shape, cuts, -0.22, 0.18) if cuts else 1.0
    array = jax.random.normal(rng, shape, jnp.float32) * scale * loudness
    return jnp.minimum(jnp.maximum(array, -reach), reach).astype(held_as)


def setup_inputs(seed: int = 0) -> dict:
    seeds = jax.random.split(jax.random.key(seed), 4)
    return {
        "velocity": scatter_about(seeds[0], (3, NZF, FBLOCKS, BLOCK_EDGE * BLOCK_EDGE), 1.0, 6.0, ((1, 24), (2, 32)), jnp.float32),
        "magnetic": scatter_about(seeds[1], (3, NZC, NYC, NXC), 1.0, 6.0, ((1, 24), (2, 32)), jnp.float32),
        "slot_block_table": draw_slot_block_table(jax.random.fold_in(seeds[3], 71), 0),
    }


def restrict(fine, blk):
    half_width = blk // 2
    s = fine.shape
    v = fine.reshape(s[0], s[1] // 2, 2, s[2], half_width, 2, half_width, 2)
    return (jnp.sum(v, axis=(2, 5, 7)) * 0.125).reshape(s[0], s[1] // 2, s[2], half_width * half_width)


def central(magnetic_state, axis):
    return (jnp.roll(magnetic_state, -1, axis) - jnp.roll(magnetic_state, 1, axis)) * 0.5


def curl(v):
    return jnp.stack([central(v[2], 1) - central(v[1], 0), central(v[0], 0) - central(v[2], 2), central(v[1], 2) - central(v[0], 1)])


def cross(a, b):
    return jnp.stack([a[1] * b[2] - a[2] * b[1], a[2] * b[0] - a[0] * b[2], a[0] * b[1] - a[1] * b[0]])


def laplace(v):
    total = -6.0 * v
    for axis in (1, 2, 3):
        total = total + jnp.roll(v, 1, axis) + jnp.roll(v, -1, axis)
    return total


def reference(velocity, magnetic, slot_block_table):
    half_width = BLOCK_EDGE // 2
    tile_stack = restrict(velocity, BLOCK_EDGE)
    sorted_positions = jnp.argsort(slot_block_table).astype(jnp.int32)
    ordered = tile_stack[:, :, sorted_positions]
    nzc = ordered.shape[1]
    grid = ordered.reshape(3, nzc, BROWS, BCOLS, half_width, half_width).transpose(0, 1, 2, 4, 3, 5).reshape(3, nzc, BROWS * half_width, BCOLS * half_width)
    emf = cross(grid, magnetic)
    current = curl(magnetic)
    magnetic_next = magnetic + 0.1 * (curl(emf) + 0.5 * laplace(magnetic))
    lorentz_force = cross(current, magnetic)
    blocks = lorentz_force.reshape(3, nzc, BROWS, half_width, BCOLS, half_width).transpose(0, 1, 2, 4, 3, 5).reshape(3, nzc, BROWS * BCOLS, half_width, half_width)
    blocks_per_slot = blocks[:, :, slot_block_table]
    n = blocks_per_slot.shape[2]
    widened_tiles = jnp.broadcast_to(blocks_per_slot.reshape(3, nzc, 1, n, half_width, 1, half_width, 1), (3, nzc, 2, n, half_width, 2, half_width, 2))
    updated_fine_velocity = velocity + 0.1 * widened_tiles.reshape(3, nzc * 2, n, BLOCK_EDGE * BLOCK_EDGE)
    return updated_fine_velocity, magnetic_next
```

```python
import functools

import jax
import jax.numpy as jnp
from jax import lax
from jax.experimental import pallas as pl
from jax.experimental.pallas import tpu as pltpu
from jax.sharding import PartitionSpec as P

MESH = pl.DeviceIdType.MESH
LANES = 128
EDGE = 16
ROWS = 12


def halves(value):
    high = value.astype(jnp.bfloat16)
    return high, (value - high.astype(jnp.float32)).astype(jnp.bfloat16)


def stacked_halves(value):
    return jnp.concatenate(halves(value), axis=0)


def dot(a, b):
    return jnp.dot(a, b, preferred_element_type=jnp.float32)


def iota(shape, dim):
    return lax.broadcasted_iota(jnp.int32, shape, dim)


def one_hot(condition):
    return jnp.where(condition, 1.0, 0.0)


def turn_chunks(tile):
    t, m = iota((8, LANES), 0), iota((8, LANES), 1) // EDGE
    skewed = pltpu.roll(tile, 0, 1, stride=EDGE, stride_axis=0)
    picked = jnp.take_along_axis(skewed, (m + t) & 7, axis=0)
    return pltpu.roll(picked, 0, 1, stride=EDGE, stride_axis=0)


def blocks_to_grid(half_rows, n):
    return jnp.concatenate(
        [
            jnp.concatenate(
                [turn_chunks(rows[8 * g : 8 * g + 8]) for g in range(n // 8)], axis=1
            )
            for rows in half_rows
        ],
        axis=0,
    )


def grid_to_blocks(plane, n):
    return [
        jnp.concatenate(
            [
                turn_chunks(plane[8 * h : 8 * h + 8, LANES * g : LANES * g + LANES])
                for g in range(n // 8)
            ],
            axis=0,
        )
        for h in range(2)
    ]


def shift_x(plane):
    width = plane.shape[1]
    return (pltpu.roll(plane, width - 1, 1), pltpu.roll(plane, 1, 1))


def shift_y(plane, low, high):
    y = iota(plane.shape, 0)
    return (
        jnp.where(y == EDGE - 1, high, pltpu.roll(plane, EDGE - 1, 0)),
        jnp.where(y == 0, low, pltpu.roll(plane, 1, 0)),
    )


def central(pair):
    return (pair[0] - pair[1]) * 0.5


def cross(a, b):
    return [
        a[1] * b[2] - a[2] * b[1],
        a[2] * b[0] - a[0] * b[2],
        a[0] * b[1] - a[1] * b[0],
    ]


def kernel(
    cols, rows, depth,
    vel, mag, table, vel_out, mag_out,
    fine, field, ids_send, ids, v_send, v_got, f_send, f_got,
    by_send, by, bz, ey_send, ey, emf, ez, mag_new,
    load_sems, out_sems, send_sems, ids_sem, v_sem, f_sem, by_sem, bz_sems, ey_sem, ez_sems,
):
    n = cols * rows
    width = EDGE * n
    me, z = lax.axis_index("xy"), lax.axis_index("gz")
    my_x, my_y = me // rows, lax.rem(me, rows)

    def peer(j):
        return lax.rem(my_x + j // rows, cols) * rows + lax.rem(my_y + j % rows, rows)

    def slot_there(j):
        return (-(j // rows)) % cols * rows + (-(j % rows)) % rows

    above, below = lax.rem(me + 1, n), lax.rem(me + n - 1, n)
    upper, lower = lax.rem(z + 1, depth), lax.rem(z + depth - 1, depth)

    loads = [pltpu.make_async_copy(mag, field, load_sems.at[3])] + [
        pltpu.make_async_copy(vel.at[c], fine.at[c], load_sems.at[c]) for c in range(3)
    ]
    for load in loads:
        load.start()

    barrier = pltpu.get_barrier_semaphore()
    for j in range(1, n):
        pl.semaphore_signal(barrier, inc=1, device_id=(peer(j), z), device_id_type=MESH)
    for other in (upper, lower):
        pl.semaphore_signal(barrier, inc=1, device_id=(me, other), device_id_type=MESH)

    own_row = table[...]
    ids_send[...] = jnp.full((1, LANES), -1, jnp.int32)
    ids_send[:, 0:n] = own_row

    f_cell, c_cell = iota((1024, 256), 0), iota((1024, 256), 1)
    c_y = c_cell // LANES * 8 + (-(c_cell // EDGE) & 7)
    to_coarse = jnp.where(
        (f_cell // 64 == c_y) & (f_cell % 32 // 2 == c_cell % 16), 0.125, 0.0
    ).astype(jnp.bfloat16)
    j_sub = iota((n, n), 0)
    peer_row = lax.rem(my_x + j_sub // rows, cols) * rows + lax.rem(my_y + j_sub % rows, rows)
    pick = one_hot(own_row // n == peer_row).astype(jnp.bfloat16)
    pick2 = jnp.concatenate([pick, pick], axis=1)

    def means(c):
        loads[1 + c].wait()
        pair = jnp.concatenate(
            [fine[c, 0] + fine[c, 1], fine[c, 2] + fine[c, 3]], axis=0
        )
        both = dot(stacked_halves(pair), to_coarse)
        mean = both[: 2 * n] + both[2 * n :]
        by_slot = jnp.concatenate([mean[:n], mean[n:]], axis=1)
        by_peer = dot(pick2, stacked_halves(by_slot))
        for k in range(4):
            v_send[:, 4 * c + k, :] = by_peer[:, LANES * k : LANES * k + LANES]

    for c in range(3):
        means(c)

    loads[0].wait()
    for p in range(6):
        by_send[0, p : p + 1, :] = field[p // 2, p % 2, EDGE - 1 : EDGE, :]
        by_send[1, p : p + 1, :] = field[p // 2, p % 2, 0:1, :]

    pl.semaphore_wait(barrier, n + 1)

    def remote(src, dst, sent, got, xy, gz):
        return pltpu.make_async_remote_copy(
            src_ref=src, dst_ref=dst, send_sem=sent, recv_sem=got,
            device_id=(xy, gz), device_id_type=MESH,
        )

    for j in range(1, n):
        remote(ids_send, ids.at[pl.ds(slot_there(j), 1)], send_sems.at[0], ids_sem, peer(j), z).start()
    edges = [
        remote(field.at[:, 1], bz.at[0], send_sems.at[1], bz_sems.at[0], me, upper),
        remote(field.at[:, 0], bz.at[1], send_sems.at[2], bz_sems.at[1], me, lower),
        remote(by_send.at[0], by.at[0], send_sems.at[3], by_sem.at[0], above, z),
        remote(by_send.at[1], by.at[1], send_sems.at[4], by_sem.at[1], below, z),
    ]
    for edge in edges:
        edge.start()
    for j in range(1, n):
        remote(v_send.at[j], v_got.at[slot_there(j)], send_sems.at[5], v_sem, peer(j), z).start()
    v_got[0] = v_send[0]
    ids[0:1, :] = ids_send[...]

    rest = pl.ds(0, n - 1)

    def wait_all(ref, sem):
        pltpu.make_async_copy(ref.at[rest], ref.at[rest], sem).wait()

    for edge in edges:
        edge.wait_recv()
    b = [[field[c, k] for k in range(2)] for c in range(3)]

    curl_terms, spread = [], []
    for c in range(3):
        along_z = [(b[c][1], bz[0, c]), (bz[1, c], b[c][0])]
        along_y = [
            shift_y(b[c][k], by[0, 2 * c + k : 2 * c + k + 1, :], by[1, 2 * c + k : 2 * c + k + 1, :])
            for k in range(2)
        ]
        along_x = [shift_x(b[c][k]) for k in range(2)]
        curl_terms.append((along_z, along_y, along_x))
        spread.append(
            [
                (along_z[k][0] + along_z[k][1])
                + (along_y[k][0] + along_y[k][1])
                + (along_x[k][0] + along_x[k][1])
                - 6.0 * b[c][k]
                for k in range(2)
            ]
        )
    force = []
    for k in range(2):
        zs, ys, xs = (
            [central(curl_terms[c][d][k]) for c in range(3)] for d in range(3)
        )
        current = [ys[2] - zs[1], zs[0] - xs[2], xs[1] - ys[0]]
        force.append([0.1 * f for f in cross(current, [b[c][k] for c in range(3)])])
    for c in range(3):
        for k in range(2):
            mag_new[c, k] = b[c][k] + 0.05 * spread[c][k]

    wait_all(ids, ids_sem)
    listed = ids[...]
    column = jnp.where((listed >= 0) & (listed // n == me), lax.rem(listed, n), 0)
    of_peer = jnp.sum(column, axis=1, keepdims=True)
    lane = iota((n, n), 1)
    turned = lane // 8 * 8 + (-lane & 7)
    give = one_hot(of_peer == turned).astype(jnp.bfloat16)
    column_row = lax.dot_general(
        jnp.ones((n, LANES), jnp.bfloat16), column.astype(jnp.float32).astype(jnp.bfloat16),
        (((1,), (1,)), ((), ())), preferred_element_type=jnp.float32,
    )
    take = one_hot(column_row == iota((n, n), 0).astype(jnp.float32)).astype(jnp.bfloat16)
    give2 = jnp.concatenate([give, give], axis=1)
    take2 = jnp.concatenate([take, take], axis=1)

    tiles = []
    for c in range(3):
        for k in range(2):
            tiles += grid_to_blocks(force[k][c], n)
    by_peer = dot(give2, stacked_halves(jnp.concatenate(tiles, axis=1)))
    for k in range(ROWS):
        f_send[:, k, :] = by_peer[:, LANES * k : LANES * k + LANES]
    for j in range(1, n):
        remote(f_send.at[j], f_got.at[slot_there(j)], send_sems.at[6], f_sem, peer(j), z).start()
    f_got[0] = f_send[0]

    wait_all(v_got, v_sem)
    blocks = dot(
        take2,
        stacked_halves(jnp.concatenate([v_got[:, k, :] for k in range(ROWS)], axis=1)),
    )
    parts = [blocks[:, LANES * k : LANES * k + LANES] for k in range(ROWS)]
    flow = [
        [blocks_to_grid(parts[4 * c + 2 * k : 4 * c + 2 * k + 2], n) for k in range(2)]
        for c in range(3)
    ]
    for k in range(2):
        e = cross([flow[c][k] for c in range(3)], [field[c, k] for c in range(3)])
        for c in range(3):
            emf[k, c] = e[c]
        for i, c in enumerate((0, 2)):
            ey_send[0, 2 * i + k : 2 * i + k + 1, :] = e[c][EDGE - 1 : EDGE, :]
            ey_send[1, 2 * i + k : 2 * i + k + 1, :] = e[c][0:1, :]
    edges2 = [
        remote(emf.at[1, pl.ds(0, 2)], ez.at[0], send_sems.at[7], ez_sems.at[0], me, upper),
        remote(emf.at[0, pl.ds(0, 2)], ez.at[1], send_sems.at[8], ez_sems.at[1], me, lower),
        remote(ey_send.at[0], ey.at[0], send_sems.at[9], ey_sem.at[0], above, z),
        remote(ey_send.at[1], ey.at[1], send_sems.at[10], ey_sem.at[1], below, z),
    ]
    for edge in edges2:
        edge.start()
    for edge in edges2:
        edge.wait_recv()

    def dz(c, k):
        return central((emf[1, c], ez[0, c]) if k == 0 else (ez[1, c], emf[0, c]))

    def dy(c, k):
        i = 2 * (c // 2) + k
        return central(shift_y(emf[k, c], ey[0, i : i + 1, :], ey[1, i : i + 1, :]))

    def dx(c, k):
        return central(shift_x(emf[k, c]))

    for k in range(2):
        mag_new[0, k] += 0.1 * (dy(2, k) - dz(1, k))
        mag_new[1, k] += 0.1 * (dz(0, k) - dx(2, k))
        mag_new[2, k] += 0.1 * (dx(1, k) - dy(0, k))
    outs = [pltpu.make_async_copy(mag_new, mag_out, out_sems.at[3])]
    outs[0].start()

    s_sub, s_lane = iota((n, n), 0), iota((n, n), 1)
    own_diagonal = jnp.where(s_sub == s_lane, own_row // n, 0).astype(jnp.float32).astype(jnp.bfloat16)
    row_of_slot = lax.dot_general(
        own_diagonal, jnp.ones((n, n), jnp.bfloat16),
        (((1,), (1,)), ((), ())), preferred_element_type=jnp.float32,
    )
    row_at = lax.rem(my_x + s_lane // rows, cols) * rows + lax.rem(my_y + s_lane % rows, rows)
    back = one_hot(row_of_slot == row_at.astype(jnp.float32)).astype(jnp.bfloat16)
    c_cell2, f_cell2 = iota((256, 1024), 0), iota((256, 1024), 1)
    to_fine = one_hot(
        (f_cell2 // 64 == c_cell2 // 16) & (f_cell2 % 32 // 2 == c_cell2 % 16)
    ).astype(jnp.bfloat16)
    wait_all(f_got, f_sem)
    for c in range(3):
        high, low = halves(
            jnp.concatenate([f_got[:, 4 * c + k, :] for k in range(4)], axis=1)
        )
        high = dot(back, high).astype(jnp.bfloat16)
        low = dot(back, low).astype(jnp.bfloat16)
        wide = dot(
            jnp.concatenate([high[:, :256], high[:, 256:], low[:, :256], low[:, 256:]], axis=0),
            to_fine,
        )
        for k in range(2):
            gain = wide[n * k : n * k + n] + wide[2 * n + n * k : 2 * n + n * k + n]
            fine[c, 2 * k] += gain
            fine[c, 2 * k + 1] += gain
        out = pltpu.make_async_copy(fine.at[c], vel_out.at[c], out_sems.at[c])
        out.start()
        outs.append(out)

    for edge in edges + edges2:
        edge.wait_send()
    pltpu.make_async_copy(ids.at[rest], ids.at[rest], send_sems.at[0]).wait()
    wait_all(v_send, send_sems.at[5])
    wait_all(f_send, send_sems.at[6])
    for out in outs:
        out.wait()


def body(cols, rows, depth, velocity, magnetic, slot_block_table):
    n = cols * rows
    width = EDGE * n
    f32 = jnp.float32
    any_place = pl.BlockSpec(memory_space=pl.ANY)
    dma = pltpu.SemaphoreType.DMA
    return pl.pallas_call(
        functools.partial(kernel, cols, rows, depth),
        out_shape=(
            jax.ShapeDtypeStruct(velocity.shape, f32),
            jax.ShapeDtypeStruct(magnetic.shape, f32),
        ),
        in_specs=[any_place, any_place, pl.BlockSpec(memory_space=pltpu.VMEM)],
        out_specs=(any_place, any_place),
        scratch_shapes=[
            pltpu.VMEM((3, 4, n, 1024), f32),
            pltpu.VMEM((3, 2, EDGE, width), f32),
            pltpu.VMEM((1, LANES), jnp.int32),
            pltpu.VMEM((n, LANES), jnp.int32),
            pltpu.VMEM((n, ROWS, LANES), f32),
            pltpu.VMEM((n, ROWS, LANES), f32),
            pltpu.VMEM((n, ROWS, LANES), f32),
            pltpu.VMEM((n, ROWS, LANES), f32),
            pltpu.VMEM((2, 6, width), f32),
            pltpu.VMEM((2, 6, width), f32),
            pltpu.VMEM((2, 3, EDGE, width), f32),
            pltpu.VMEM((2, 4, width), f32),
            pltpu.VMEM((2, 4, width), f32),
            pltpu.VMEM((2, 3, EDGE, width), f32),
            pltpu.VMEM((2, 2, EDGE, width), f32),
            pltpu.VMEM((3, 2, EDGE, width), f32),
            dma((4,)), dma((4,)), dma((11,)), dma, dma, dma,
            dma((2,)), dma((2,)), dma((2,)), dma((2,)),
        ],
        compiler_params=pltpu.CompilerParams(
            collective_id=0, has_side_effects=True, vmem_limit_bytes=48 << 20
        ),
        name="dynamo_substep",
    )(velocity, magnetic, slot_block_table.reshape(1, n))


def solution(mesh):
    n, depth = mesh.shape["xy"], mesh.shape["gz"]
    rows = {32: 8, 8: 4}[n]
    spec = P(None, "gz", "xy", None)
    return jax.shard_map(
        functools.partial(body, n // rows, rows, depth),
        mesh=mesh,
        in_specs=(spec, spec, P("xy")),
        out_specs=(spec, spec),
        check_vma=False,
    )
```

```python
import functools

import jax
import jax.numpy as jnp
from jax import lax
from jax.experimental import pallas as pl
from jax.experimental.pallas import tpu as pltpu
from jax.sharding import PartitionSpec as P

MESH = pl.DeviceIdType.MESH
LANES = 128
EDGE = 16
ROWS = 12


def halves(value):
    high = value.astype(jnp.bfloat16)
    return high, (value - high.astype(jnp.float32)).astype(jnp.bfloat16)


def stacked_halves(value):
    return jnp.concatenate(halves(value), axis=0)


def dot(a, b):
    return jnp.dot(a, b, preferred_element_type=jnp.float32)


def iota(shape, dim):
    return lax.broadcasted_iota(jnp.int32, shape, dim)


def one_hot(condition):
    return jnp.where(condition, 1.0, 0.0)


def turn_chunks(tile):
    t, m = iota((8, LANES), 0), iota((8, LANES), 1) // EDGE
    skewed = pltpu.roll(tile, 0, 1, stride=EDGE, stride_axis=0)
    picked = jnp.take_along_axis(skewed, (m + t) & 7, axis=0)
    return pltpu.roll(picked, 0, 1, stride=EDGE, stride_axis=0)


def blocks_to_grid(half_rows, n):
    return jnp.concatenate(
        [
            jnp.concatenate(
                [turn_chunks(rows[8 * g : 8 * g + 8]) for g in range(n // 8)], axis=1
            )
            for rows in half_rows
        ],
        axis=0,
    )


def grid_to_blocks(plane, n):
    return [
        jnp.concatenate(
            [
                turn_chunks(plane[8 * h : 8 * h + 8, LANES * g : LANES * g + LANES])
                for g in range(n // 8)
            ],
            axis=0,
        )
        for h in range(2)
    ]


def shift_x(plane):
    width = plane.shape[1]
    return (pltpu.roll(plane, width - 1, 1), pltpu.roll(plane, 1, 1))


def shift_y(plane, low, high):
    y = iota(plane.shape, 0)
    return (
        jnp.where(y == EDGE - 1, high, pltpu.roll(plane, EDGE - 1, 0)),
        jnp.where(y == 0, low, pltpu.roll(plane, 1, 0)),
    )


def central(pair):
    return (pair[0] - pair[1]) * 0.5


def cross(a, b):
    return [
        a[1] * b[2] - a[2] * b[1],
        a[2] * b[0] - a[0] * b[2],
        a[0] * b[1] - a[1] * b[0],
    ]


def kernel(
    cols, rows, depth,
    vel, mag, table, fine, mag_new,
    field, own, v_send, v_got, f_send, f_got,
    by_send, by, bz, ey_send, ey, emf, ez,
    load_sems, send_sems, v_sem, f_sem, by_sem, bz_sems, ey_sem, ez_sems,
):
    n = cols * rows
    width = EDGE * n
    me, z = lax.axis_index("xy"), lax.axis_index("gz")
    my_x, my_y = me // rows, lax.rem(me, rows)

    def peer(j):
        return lax.rem(my_x + j // rows, cols) * rows + lax.rem(my_y + j % rows, rows)

    def slot_there(j):
        return (-(j // rows)) % cols * rows + (-(j % rows)) % rows

    above, below = lax.rem(me + 1, n), lax.rem(me + n - 1, n)
    upper, lower = lax.rem(z + 1, depth), lax.rem(z + depth - 1, depth)

    loads = [
        pltpu.make_async_copy(table, own, load_sems.at[0]),
        *(pltpu.make_async_copy(vel.at[c], fine.at[c], load_sems.at[1 + c]) for c in range(3)),
        pltpu.make_async_copy(mag, field, load_sems.at[4]),
    ]
    for load in loads:
        load.start()

    barrier = pltpu.get_barrier_semaphore()
    for j in range(1, n):
        pl.semaphore_signal(barrier, inc=1, device_id=(peer(j), z), device_id_type=MESH)
    pl.semaphore_signal(barrier, inc=1, device_id=(me, lower), device_id_type=MESH)

    f_cell, c_cell = iota((1024, 256), 0), iota((1024, 256), 1)
    c_y = c_cell // LANES * 8 + (-(c_cell // EDGE) & 7)
    to_coarse = jnp.where(
        (f_cell // 64 == c_y) & (f_cell % 32 // 2 == c_cell % 16), 0.125, 0.0
    ).astype(jnp.bfloat16)
    loads[0].wait()
    own_row = own[...]
    j_sub = iota((n, n), 0)
    peer_row = lax.rem(my_x + j_sub // rows, cols) * rows + lax.rem(my_y + j_sub % rows, rows)
    pick = one_hot(own_row // n == peer_row)
    columns = jnp.sum(pick * lax.rem(own_row, n).astype(jnp.float32), axis=1, keepdims=True)
    v_send[:, ROWS, :] = jnp.broadcast_to(columns, (n, LANES))
    pick = pick.astype(jnp.bfloat16)
    pick2 = jnp.concatenate([pick, pick], axis=1)

    def means(c):
        loads[1 + c].wait()
        pair = jnp.concatenate(
            [fine[c, 0] + fine[c, 1], fine[c, 2] + fine[c, 3]], axis=0
        )
        both = dot(stacked_halves(pair), to_coarse)
        mean = both[: 2 * n] + both[2 * n :]
        by_slot = jnp.concatenate([mean[:n], mean[n:]], axis=1)
        by_peer = dot(pick2, stacked_halves(by_slot))
        for k in range(4):
            v_send[:, 4 * c + k, :] = by_peer[:, LANES * k : LANES * k + LANES]

    for c in range(3):
        means(c)

    loads[4].wait()
    for p in range(6):
        by_send[0, p : p + 1, :] = field[p // 2, p % 2, EDGE - 1 : EDGE, :]
        by_send[1, p : p + 1, :] = field[p // 2, p % 2, 0:1, :]

    pl.semaphore_wait(barrier, n)

    def remote(src, dst, sent, got, xy, gz):
        return pltpu.make_async_remote_copy(
            src_ref=src, dst_ref=dst, send_sem=sent, recv_sem=got,
            device_id=(xy, gz), device_id_type=MESH,
        )

    up = remote(field.at[:, 1], bz.at[0], send_sems.at[1], bz_sems.at[0], me, upper)
    down = remote(field.at[:, 0], bz.at[1], send_sems.at[2], bz_sems.at[1], me, lower)
    edges = [
        remote(by_send.at[0], by.at[0], send_sems.at[3], by_sem.at[0], above, z),
        remote(by_send.at[1], by.at[1], send_sems.at[4], by_sem.at[1], below, z),
    ]
    up.start()
    for edge in edges:
        edge.start()
    for j in range(1, n):
        remote(v_send.at[j], v_got.at[slot_there(j)], send_sems.at[5], v_sem, peer(j), z).start()
    v_got[0] = v_send[0]

    rest = pl.ds(0, n - 1)

    def wait_all(ref, sem):
        pltpu.make_async_copy(ref.at[rest], ref.at[rest], sem).wait()

    up.wait_recv()
    down.start()
    down.wait_recv()
    for edge in edges:
        edge.wait_recv()
    b = [[field[c, k] for k in range(2)] for c in range(3)]

    curl_terms, spread = [], []
    for c in range(3):
        along_z = [(b[c][1], bz[0, c]), (bz[1, c], b[c][0])]
        along_y = [
            shift_y(b[c][k], by[0, 2 * c + k : 2 * c + k + 1, :], by[1, 2 * c + k : 2 * c + k + 1, :])
            for k in range(2)
        ]
        along_x = [shift_x(b[c][k]) for k in range(2)]
        curl_terms.append((along_z, along_y, along_x))
        spread.append(
            [
                (along_z[k][0] + along_z[k][1])
                + (along_y[k][0] + along_y[k][1])
                + (along_x[k][0] + along_x[k][1])
                - 6.0 * b[c][k]
                for k in range(2)
            ]
        )
    force = []
    for k in range(2):
        zs, ys, xs = (
            [central(curl_terms[c][d][k]) for c in range(3)] for d in range(3)
        )
        current = [ys[2] - zs[1], zs[0] - xs[2], xs[1] - ys[0]]
        force.append([0.1 * f for f in cross(current, [b[c][k] for c in range(3)])])
    for c in range(3):
        for k in range(2):
            mag_new[c, k] = b[c][k] + 0.05 * spread[c][k]

    wait_all(v_got, v_sem)
    of_peer = v_got[:, ROWS, 0:n]
    column_row = lax.dot_general(
        jnp.ones((n, n), jnp.bfloat16), (of_peer * (1.0 / n)).astype(jnp.bfloat16),
        (((1,), (1,)), ((), ())), preferred_element_type=jnp.float32,
    )
    take = one_hot(column_row == iota((n, n), 0).astype(jnp.float32)).astype(jnp.bfloat16)
    take2 = jnp.concatenate([take, take], axis=1)
    blocks = dot(
        take2,
        stacked_halves(jnp.concatenate([v_got[:, k, :] for k in range(ROWS)], axis=1)),
    )
    parts = [blocks[:, LANES * k : LANES * k + LANES] for k in range(ROWS)]
    flow = [
        [blocks_to_grid(parts[4 * c + 2 * k : 4 * c + 2 * k + 2], n) for k in range(2)]
        for c in range(3)
    ]
    for k in range(2):
        e = cross([flow[c][k] for c in range(3)], [field[c, k] for c in range(3)])
        for c in range(3):
            emf[k, c] = e[c]
        for i, c in enumerate((0, 2)):
            ey_send[0, 2 * i + k : 2 * i + k + 1, :] = e[c][EDGE - 1 : EDGE, :]
            ey_send[1, 2 * i + k : 2 * i + k + 1, :] = e[c][0:1, :]
    edges2 = [
        remote(emf.at[1, pl.ds(0, 2)], ez.at[0], send_sems.at[7], ez_sems.at[0], me, upper),
        remote(emf.at[0, pl.ds(0, 2)], ez.at[1], send_sems.at[8], ez_sems.at[1], me, lower),
        remote(ey_send.at[0], ey.at[0], send_sems.at[9], ey_sem.at[0], above, z),
        remote(ey_send.at[1], ey.at[1], send_sems.at[10], ey_sem.at[1], below, z),
    ]
    for edge in edges2:
        edge.start()
    lane = iota((n, n), 1)
    turned = lane // 8 * 8 + (-lane & 7)
    give = one_hot(of_peer == turned.astype(jnp.float32)).astype(jnp.bfloat16)
    give2 = jnp.concatenate([give, give], axis=1)
    tiles = []
    for c in range(3):
        for k in range(2):
            tiles += grid_to_blocks(force[k][c], n)
    by_peer = dot(give2, stacked_halves(jnp.concatenate(tiles, axis=1)))
    for k in range(ROWS):
        f_send[:, k, :] = by_peer[:, LANES * k : LANES * k + LANES]
    for j in range(1, n):
        remote(f_send.at[j], f_got.at[slot_there(j)], send_sems.at[6], f_sem, peer(j), z).start()
    f_got[0] = f_send[0]

    s_sub, s_lane = iota((n, n), 0), iota((n, n), 1)
    own_diagonal = jnp.where(s_sub == s_lane, own_row // n, 0).astype(jnp.float32).astype(jnp.bfloat16)
    row_of_slot = lax.dot_general(
        own_diagonal, jnp.ones((n, n), jnp.bfloat16),
        (((1,), (1,)), ((), ())), preferred_element_type=jnp.float32,
    )
    row_at = lax.rem(my_x + s_lane // rows, cols) * rows + lax.rem(my_y + s_lane % rows, rows)
    back = one_hot(row_of_slot == row_at.astype(jnp.float32)).astype(jnp.bfloat16)
    c_cell2, f_cell2 = iota((256, 1024), 0), iota((256, 1024), 1)
    to_fine = one_hot(
        (f_cell2 // 64 == c_cell2 // 16) & (f_cell2 % 32 // 2 == c_cell2 % 16)
    ).astype(jnp.bfloat16)
    wait_all(f_got, f_sem)
    for c in range(3):
        high, low = halves(
            jnp.concatenate([f_got[:, 4 * c + k, :] for k in range(4)], axis=1)
        )
        high = dot(back, high).astype(jnp.bfloat16)
        low = dot(back, low).astype(jnp.bfloat16)
        wide = dot(
            jnp.concatenate([high[:, :256], high[:, 256:], low[:, :256], low[:, 256:]], axis=0),
            to_fine,
        )
        for k in range(2):
            gain = wide[n * k : n * k + n] + wide[2 * n + n * k : 2 * n + n * k + n]
            fine[c, 2 * k] += gain
            fine[c, 2 * k + 1] += gain

    for edge in edges2:
        edge.wait_recv()

    def dz(c, k):
        return central((emf[1, c], ez[0, c]) if k == 0 else (ez[1, c], emf[0, c]))

    def dy(c, k):
        i = 2 * (c // 2) + k
        return central(shift_y(emf[k, c], ey[0, i : i + 1, :], ey[1, i : i + 1, :]))

    def dx(c, k):
        return central(shift_x(emf[k, c]))

    for k in range(2):
        mag_new[0, k] += 0.1 * (dy(2, k) - dz(1, k))
        mag_new[1, k] += 0.1 * (dz(0, k) - dx(2, k))
        mag_new[2, k] += 0.1 * (dx(1, k) - dy(0, k))

    for edge in [up, down] + edges + edges2:
        edge.wait_send()
    wait_all(v_send, send_sems.at[5])
    wait_all(f_send, send_sems.at[6])


def write_out(fine, mag_new, vel_out, mag_out, sems):
    copies = [
        pltpu.make_async_copy(fine, vel_out, sems.at[0]),
        pltpu.make_async_copy(mag_new, mag_out, sems.at[1]),
    ]
    for copy in copies:
        copy.start()
    for copy in copies:
        copy.wait()


def body(cols, rows, depth, velocity, magnetic, slot_block_table):
    n = cols * rows
    width = EDGE * n
    f32 = jnp.float32
    far = pl.BlockSpec(memory_space=pl.ANY)
    near = pl.BlockSpec(memory_space=pltpu.VMEM)
    dma = pltpu.SemaphoreType.DMA
    fine, mag_new = pl.pallas_call(
        functools.partial(kernel, cols, rows, depth),
        out_shape=(
            pltpu.VMEM(velocity.shape, f32),
            pltpu.VMEM(magnetic.shape, f32),
        ),
        in_specs=[far, far, far],
        out_specs=(near, near),
        scratch_shapes=[
            pltpu.VMEM((3, 2, EDGE, width), f32),
            pltpu.VMEM((1, n), jnp.int32),
            pltpu.VMEM((n, ROWS + 1, LANES), f32),
            pltpu.VMEM((n, ROWS + 1, LANES), f32),
            pltpu.VMEM((n, ROWS, LANES), f32),
            pltpu.VMEM((n, ROWS, LANES), f32),
            pltpu.VMEM((2, 6, width), f32),
            pltpu.VMEM((2, 6, width), f32),
            pltpu.VMEM((2, 3, EDGE, width), f32),
            pltpu.VMEM((2, 4, width), f32),
            pltpu.VMEM((2, 4, width), f32),
            pltpu.VMEM((2, 3, EDGE, width), f32),
            pltpu.VMEM((2, 2, EDGE, width), f32),
            dma((5,)), dma((11,)), dma, dma, dma((2,)), dma((2,)), dma((2,)), dma((2,)),
        ],
        compiler_params=pltpu.CompilerParams(
            collective_id=0, has_side_effects=True, vmem_limit_bytes=60 << 20
        ),
        name="dynamo_substep",
    )(velocity, magnetic, slot_block_table.reshape(1, n))
    return pl.pallas_call(
        write_out,
        out_shape=(
            jax.ShapeDtypeStruct(velocity.shape, f32),
            jax.ShapeDtypeStruct(magnetic.shape, f32),
        ),
        in_specs=[near, near],
        out_specs=(far, far),
        scratch_shapes=[dma((2,))],
        name="write_out",
    )(*(pltpu.with_memory_space_constraint(a, pltpu.VMEM) for a in (fine, mag_new)))


def solution(mesh):
    n, depth = mesh.shape["xy"], mesh.shape["gz"]
    rows = {32: 8, 8: 4}[n]
    spec = P(None, "gz", "xy", None)
    return jax.shard_map(
        functools.partial(body, n // rows, rows, depth),
        mesh=mesh,
        in_specs=(spec, spec, P("xy")),
        out_specs=(spec, spec),
        check_vma=False,
    )
```

```python
import functools

import jax
import jax.numpy as jnp
from jax import lax
from jax.experimental import pallas as pl
from jax.experimental.pallas import tpu as pltpu
from jax.sharding import PartitionSpec as P

MESH = pl.DeviceIdType.MESH
LANES = 128
EDGE = 16
ROWS = 12


def halves(value):
    high = value.astype(jnp.bfloat16)
    return high, (value - high.astype(jnp.float32)).astype(jnp.bfloat16)


def stacked_halves(value):
    return jnp.concatenate(halves(value), axis=0)


def dot(a, b):
    return jnp.dot(a, b, preferred_element_type=jnp.float32)


def iota(shape, dim):
    return lax.broadcasted_iota(jnp.int32, shape, dim)


def one_hot(condition):
    return jnp.where(condition, 1.0, 0.0)


def turn_chunks(tile):
    t, m = iota((8, LANES), 0), iota((8, LANES), 1) // EDGE
    skewed = pltpu.roll(tile, 0, 1, stride=EDGE, stride_axis=0)
    picked = jnp.take_along_axis(skewed, (m + t) & 7, axis=0)
    return pltpu.roll(picked, 0, 1, stride=EDGE, stride_axis=0)


def blocks_to_grid(half_rows, n):
    return jnp.concatenate(
        [
            jnp.concatenate(
                [turn_chunks(rows[8 * g : 8 * g + 8]) for g in range(n // 8)], axis=1
            )
            for rows in half_rows
        ],
        axis=0,
    )


def grid_to_blocks(plane, n):
    return [
        jnp.concatenate(
            [
                turn_chunks(plane[8 * h : 8 * h + 8, LANES * g : LANES * g + LANES])
                for g in range(n // 8)
            ],
            axis=0,
        )
        for h in range(2)
    ]


def shift_x(plane):
    width = plane.shape[1]
    return (pltpu.roll(plane, width - 1, 1), pltpu.roll(plane, 1, 1))


def shift_y(plane, low, high):
    y = iota(plane.shape, 0)
    return (
        jnp.where(y == EDGE - 1, high, pltpu.roll(plane, EDGE - 1, 0)),
        jnp.where(y == 0, low, pltpu.roll(plane, 1, 0)),
    )


def central(pair):
    return (pair[0] - pair[1]) * 0.5


def cross(a, b):
    return [
        a[1] * b[2] - a[2] * b[1],
        a[2] * b[0] - a[0] * b[2],
        a[0] * b[1] - a[1] * b[0],
    ]


def kernel(
    cols, rows, depth,
    vel, mag, table, fine, mag_new,
    field, own, v_send, v_got, w_got, f_send, f_got,
    by_send, by, bz, ey_send, ey, emf, ez,
    load_sems, send_sems, entered, v_sem, w_sem, f_sem, by_sem, bz_sems, ey_sem, ez_sems,
):
    n = cols * rows
    me, z = lax.axis_index("xy"), lax.axis_index("gz")
    first, last = z == 0, z == depth - 1

    turn = jnp.where(first, 1, 0)

    def in_order(q):
        q = lax.rem(q + turn, n)
        y = q // cols
        return lax.rem(q, cols) * rows + jnp.where(2 * y < rows, y, 3 * rows // 2 - 1 - y)

    my_y = lax.rem(me, rows)
    order = jnp.where(2 * my_y < rows, my_y, 3 * rows // 2 - 1 - my_y) * cols + me // rows
    order = lax.rem(order + n - turn, n)

    def at_offset(j):
        return lax.rem(me // rows + j // rows, cols) * rows + lax.rem(my_y + j % rows, rows)

    above, below = lax.rem(me + 1, n), lax.rem(me + n - 1, n)
    upper, lower = lax.rem(z + 1, depth), lax.rem(z + depth - 1, depth)

    loads = [
        pltpu.make_async_copy(table, own, load_sems.at[0]),
        *(pltpu.make_async_copy(vel.at[c], fine.at[c], load_sems.at[1 + c]) for c in range(3)),
        pltpu.make_async_copy(mag, field, load_sems.at[4]),
    ]

    barrier = pltpu.get_barrier_semaphore()

    def greet(xy, gz):
        pl.semaphore_signal(barrier, inc=1, device_id=(xy, gz), device_id_type=MESH)

    @pl.loop(order + 1, n)
    def _(q):
        greet(in_order(q), z)

    @pl.when(jnp.logical_not(last))
    def _():
        greet(me, upper)

    @pl.when(first)
    def _():
        @pl.loop(0, n)
        def _(xy):
            greet(xy, lower)

    loads[4].start()
    for load in loads[:4]:
        load.start()
    greetings = order + jnp.where(first, 0, 1) + jnp.where(last, n, 0)

    @pl.when(greetings > 0)
    def _():
        pl.semaphore_wait(barrier, greetings)

    @pl.loop(0, order)
    def _(q):
        pl.semaphore_signal(
            entered.at[me], inc=1, device_id=(in_order(q), z), device_id_type=MESH
        )

    def remote(src, dst, sent, got, xy, gz):
        return pltpu.make_async_remote_copy(
            src_ref=src, dst_ref=dst, send_sem=sent, recv_sem=got,
            device_id=(xy, gz), device_id_type=MESH,
        )

    up = remote(field.at[:, 1], bz.at[0], send_sems.at[1], bz_sems.at[0], me, upper)
    down = remote(field.at[:, 0], bz.at[1], send_sems.at[2], bz_sems.at[1], me, lower)
    edges = [
        remote(by_send.at[0], by.at[0], send_sems.at[3], by_sem.at[0], above, z),
        remote(by_send.at[1], by.at[1], send_sems.at[4], by_sem.at[1], below, z),
    ]
    loads[4].wait()

    @pl.when(last)
    def _():
        up.start()

    @pl.when(jnp.logical_not(first))
    def _():
        down.start()

    f_cell, c_cell = iota((1024, 256), 0), iota((1024, 256), 1)
    c_y = c_cell // LANES * 8 + (-(c_cell // EDGE) & 7)
    to_coarse = jnp.where(
        (f_cell // 64 == c_y) & (f_cell % 32 // 2 == c_cell % 16), 0.125, 0.0
    ).astype(jnp.bfloat16)
    loads[0].wait()
    own_row = own[...]
    pick = one_hot(own_row // n == iota((n, n), 0))
    columns = jnp.sum(pick * lax.rem(own_row, n).astype(jnp.float32), axis=1, keepdims=True)
    v_send[:, ROWS, :] = jnp.broadcast_to(columns, (n, LANES))
    pick = pick.astype(jnp.bfloat16)
    pick2 = jnp.concatenate([pick, pick], axis=1)

    for c in range(3):
        loads[1 + c].wait()
        pair = jnp.concatenate(
            [fine[c, 0] + fine[c, 1], fine[c, 2] + fine[c, 3]], axis=0
        )
        both = dot(stacked_halves(pair), to_coarse)
        mean = both[: 2 * n] + both[2 * n :]
        by_slot = jnp.concatenate([mean[:n], mean[n:]], axis=1)
        by_peer = dot(pick2, stacked_halves(by_slot))
        for k in range(2):
            for h in range(2):
                at = LANES * (2 * k + h)
                v_send[:, 6 * k + 2 * c + h, :] = by_peer[:, at : at + LANES]

    def send_v(xy):
        remote(v_send.at[xy], v_got.at[me], send_sems.at[5], v_sem, xy, z).start()

    upper_rows = pl.ds(6, 6)

    @pl.when(last)
    def _():
        @pl.loop(0, n)
        def _(xy):
            remote(v_send.at[xy, upper_rows], w_got.at[me], send_sems.at[0], w_sem, xy, upper).start()

    @pl.loop(0, order)
    def _(q):
        send_v(in_order(q))

    for p in range(6):
        by_send[0, p : p + 1, :] = field[p // 2, p % 2, EDGE - 1 : EDGE, :]
        by_send[1, p : p + 1, :] = field[p // 2, p % 2, 0:1, :]
    v_got[me] = v_send[me]

    @pl.loop(order + 1, n)
    def _(q):
        xy = in_order(q)
        pl.semaphore_wait(entered.at[xy], 1)
        send_v(xy)

    for edge in edges:
        edge.start()

    @pl.when(jnp.logical_not(last))
    def _():
        down.wait_recv()
        up.start()

    def wait_all(ref, sem):
        rest = ref.at[pl.ds(0, n - 1)]
        pltpu.make_async_copy(rest, rest, sem).wait()

    wait_all(v_got, v_sem)
    of_peer = v_got[:, ROWS, 0:n]
    column_row = lax.dot_general(
        jnp.ones((n, n), jnp.bfloat16), (of_peer * (1.0 / n)).astype(jnp.bfloat16),
        (((1,), (1,)), ((), ())), preferred_element_type=jnp.float32,
    )
    take = one_hot(column_row == iota((n, n), 0).astype(jnp.float32)).astype(jnp.bfloat16)
    take2 = jnp.concatenate([take, take], axis=1)

    def on_grid(ref, planes):
        together = jnp.concatenate([ref[:, r, :] for r in range(6 * planes)], axis=1)
        blocks = dot(take2, stacked_halves(together))
        parts = [blocks[:, LANES * r : LANES * r + LANES] for r in range(6 * planes)]
        return [
            [blocks_to_grid(parts[6 * k + 2 * c : 6 * k + 2 * c + 2], n) for c in range(3)]
            for k in range(planes)
        ]

    flow = on_grid(v_got, 2)
    for k in range(2):
        e = cross(flow[k], [field[c, k] for c in range(3)])
        for c in range(3):
            emf[k, c] = e[c]
        for i, c in enumerate((0, 2)):
            ey_send[0, 2 * i + k : 2 * i + k + 1, :] = e[c][EDGE - 1 : EDGE, :]
            ey_send[1, 2 * i + k : 2 * i + k + 1, :] = e[c][0:1, :]
    up2 = remote(emf.at[1, pl.ds(0, 2)], ez.at[0], send_sems.at[7], ez_sems.at[0], me, upper)
    down2 = remote(emf.at[0, pl.ds(0, 2)], ez.at[1], send_sems.at[8], ez_sems.at[1], me, lower)
    edges2 = [
        remote(ey_send.at[0], ey.at[0], send_sems.at[9], ey_sem.at[0], above, z),
        remote(ey_send.at[1], ey.at[1], send_sems.at[10], ey_sem.at[1], below, z),
    ]

    @pl.when(jnp.logical_not(last))
    def _():
        up2.start()

    @pl.when(jnp.logical_not(first))
    def _():
        down2.start()

    for edge in edges2:
        edge.start()

    up.wait_recv()

    @pl.when(first)
    def _():
        down.start()
        down2.start()

    @pl.when(last)
    def _():
        down.wait_recv()

    for edge in edges:
        edge.wait_recv()

    b = [[field[c, k] for k in range(2)] for c in range(3)]
    pairs, spread = [], []
    for c in range(3):
        along_z = [(b[c][1], bz[0, c]), (bz[1, c], b[c][0])]
        along_y = [
            shift_y(b[c][k], by[0, 2 * c + k : 2 * c + k + 1, :], by[1, 2 * c + k : 2 * c + k + 1, :])
            for k in range(2)
        ]
        along_x = [shift_x(b[c][k]) for k in range(2)]
        pairs.append((along_z, along_y, along_x))
        spread.append(
            [
                (along_z[k][0] + along_z[k][1])
                + (along_y[k][0] + along_y[k][1])
                + (along_x[k][0] + along_x[k][1])
                - 6.0 * b[c][k]
                for k in range(2)
            ]
        )
    force = []
    for k in range(2):
        zs, ys, xs = ([central(pairs[c][d][k]) for c in range(3)] for d in range(3))
        current = [ys[2] - zs[1], zs[0] - xs[2], xs[1] - ys[0]]
        force.append([0.1 * f for f in cross(current, [b[c][k] for c in range(3)])])

    lane = iota((n, n), 1)
    turned = lane // 8 * 8 + (-lane & 7)
    give = one_hot(of_peer == turned.astype(jnp.float32)).astype(jnp.bfloat16)
    give2 = jnp.concatenate([give, give], axis=1)
    tiles = []
    for c in range(3):
        for k in range(2):
            tiles += grid_to_blocks(force[k][c], n)
    by_peer = dot(give2, stacked_halves(jnp.concatenate(tiles, axis=1)))
    for r in range(ROWS):
        f_send[:, r, :] = by_peer[:, LANES * r : LANES * r + LANES]

    def hops(j):
        return min(j // rows, cols - j // rows) + min(j % rows, rows - j % rows)

    for j in sorted(range(1, n), key=hops, reverse=True):
        xy = at_offset(j)
        remote(f_send.at[xy], f_got.at[me], send_sems.at[6], f_sem, xy, z).start()
    f_got[me] = f_send[me]
    for c in range(3):
        for k in range(2):
            mag_new[c, k] = b[c][k] + 0.05 * spread[c][k]

    s_sub, s_lane = iota((n, n), 0), iota((n, n), 1)
    own_diagonal = jnp.where(s_sub == s_lane, own_row // n, 0).astype(jnp.float32).astype(jnp.bfloat16)
    row_of_slot = lax.dot_general(
        own_diagonal, jnp.ones((n, n), jnp.bfloat16),
        (((1,), (1,)), ((), ())), preferred_element_type=jnp.float32,
    )
    back = one_hot(row_of_slot == s_lane.astype(jnp.float32)).astype(jnp.bfloat16)
    c_cell2, f_cell2 = iota((256, 1024), 0), iota((256, 1024), 1)
    to_fine = one_hot(
        (f_cell2 // 64 == c_cell2 // 16) & (f_cell2 % 32 // 2 == c_cell2 % 16)
    ).astype(jnp.bfloat16)

    def update():
        wait_all(f_got, f_sem)
        for c in range(3):
            high, low = halves(
                jnp.concatenate([f_got[:, 4 * c + r, :] for r in range(4)], axis=1)
            )
            high = dot(back, high).astype(jnp.bfloat16)
            low = dot(back, low).astype(jnp.bfloat16)
            wide = dot(
                jnp.concatenate([high[:, :256], high[:, 256:], low[:, :256], low[:, 256:]], axis=0),
                to_fine,
            )
            for k in range(2):
                gain = wide[n * k : n * k + n] + wide[2 * n + n * k : 2 * n + n * k + n]
                fine[c, 2 * k] += gain
                fine[c, 2 * k + 1] += gain

    def finish():
        @pl.when(jnp.logical_not(first))
        def _():
            up2.wait_recv()

        @pl.when(first)
        def _():
            every = w_got.at[:]
            pltpu.make_async_copy(every, every, w_sem).wait()
            [below_flow] = on_grid(w_got, 1)
            e = cross(below_flow, [bz[0, c] for c in range(3)])
            for c in range(2):
                ez[0, c] = e[c]

        down2.wait_recv()
        for edge in edges2:
            edge.wait_recv()

        def dz(c, k):
            return central((emf[1, c], ez[0, c]) if k == 0 else (ez[1, c], emf[0, c]))

        def dy(c, k):
            i = 2 * (c // 2) + k
            return central(shift_y(emf[k, c], ey[0, i : i + 1, :], ey[1, i : i + 1, :]))

        def dx(c, k):
            return central(shift_x(emf[k, c]))

        for k in range(2):
            mag_new[0, k] += 0.1 * (dy(2, k) - dz(1, k))
            mag_new[1, k] += 0.1 * (dz(0, k) - dx(2, k))
            mag_new[2, k] += 0.1 * (dx(1, k) - dy(0, k))

    update()
    finish()

    for edge in [up, down, down2, *edges, *edges2]:
        edge.wait_send()

    @pl.when(jnp.logical_not(last))
    def _():
        up2.wait_send()

    @pl.when(last)
    def _():
        every = w_got.at[:]
        pltpu.make_async_copy(every, every, send_sems.at[0]).wait()

    wait_all(v_send, send_sems.at[5])
    wait_all(f_send, send_sems.at[6])


def write_out(fine, mag_new, vel_out, mag_out, sems):
    copies = [
        pltpu.make_async_copy(fine, vel_out, sems.at[0]),
        pltpu.make_async_copy(mag_new, mag_out, sems.at[1]),
    ]
    for copy in copies:
        copy.start()
    for copy in copies:
        copy.wait()


def body(cols, rows, depth, velocity, magnetic, slot_block_table):
    n = cols * rows
    width = EDGE * n
    f32 = jnp.float32
    far = pl.BlockSpec(memory_space=pl.ANY)
    near = pl.BlockSpec(memory_space=pltpu.VMEM)
    dma = pltpu.SemaphoreType.DMA
    fine, mag_new = pl.pallas_call(
        functools.partial(kernel, cols, rows, depth),
        out_shape=(
            pltpu.VMEM(velocity.shape, f32),
            pltpu.VMEM(magnetic.shape, f32),
        ),
        in_specs=[far, far, far],
        out_specs=(near, near),
        scratch_shapes=[
            pltpu.VMEM((3, 2, EDGE, width), f32),
            pltpu.VMEM((1, n), jnp.int32),
            pltpu.VMEM((n, ROWS + 1, LANES), f32),
            pltpu.VMEM((n, ROWS + 1, LANES), f32),
            pltpu.VMEM((n, 6, LANES), f32),
            pltpu.VMEM((n, ROWS, LANES), f32),
            pltpu.VMEM((n, ROWS, LANES), f32),
            pltpu.VMEM((2, 6, width), f32),
            pltpu.VMEM((2, 6, width), f32),
            pltpu.VMEM((2, 3, EDGE, width), f32),
            pltpu.VMEM((2, 4, width), f32),
            pltpu.VMEM((2, 4, width), f32),
            pltpu.VMEM((2, 3, EDGE, width), f32),
            pltpu.VMEM((2, 2, EDGE, width), f32),
            dma((5,)), dma((11,)), pltpu.SemaphoreType.REGULAR((n,)), dma, dma, dma, dma((2,)), dma((2,)), dma((2,)), dma((2,)),
        ],
        compiler_params=pltpu.CompilerParams(
            collective_id=0, has_side_effects=True, vmem_limit_bytes=60 << 20
        ),
        name="dynamo_substep",
    )(velocity, magnetic, slot_block_table.reshape(1, n))
    return pl.pallas_call(
        write_out,
        out_shape=(
            jax.ShapeDtypeStruct(velocity.shape, f32),
            jax.ShapeDtypeStruct(magnetic.shape, f32),
        ),
        in_specs=[near, near],
        out_specs=(far, far),
        scratch_shapes=[dma((2,))],
        name="write_out",
    )(*(pltpu.with_memory_space_constraint(a, pltpu.VMEM) for a in (fine, mag_new)))


def solution(mesh):
    n, depth = mesh.shape["xy"], mesh.shape["gz"]
    rows = {32: 8, 8: 4}[n]
    spec = P(None, "gz", "xy", None)
    return jax.shard_map(
        functools.partial(body, n // rows, rows, depth),
        mesh=mesh,
        in_specs=(spec, spec, P("xy")),
        out_specs=(spec, spec),
        check_vma=False,
    )
```

```python
import functools

import jax
import jax.numpy as jnp
from jax import lax
from jax.experimental import pallas as pl
from jax.experimental.pallas import tpu as pltpu
from jax.sharding import PartitionSpec as P

MESH = pl.DeviceIdType.MESH
LANES = 128
EDGE = 16
ROWS = 12
HALF_ROWS = 6


def halves(value):
    high = value.astype(jnp.bfloat16)
    return high, (value - high.astype(jnp.float32)).astype(jnp.bfloat16)


def stacked_halves(value):
    return jnp.concatenate(halves(value), axis=0)


def dot(a, b):
    return jnp.dot(a, b, preferred_element_type=jnp.float32)


def iota(shape, dim):
    return lax.broadcasted_iota(jnp.int32, shape, dim)


def one_hot(condition):
    return jnp.where(condition, 1.0, 0.0)


def turn_chunks(tile):
    t, m = iota((8, LANES), 0), iota((8, LANES), 1) // EDGE
    skewed = pltpu.roll(tile, 0, 1, stride=EDGE, stride_axis=0)
    picked = jnp.take_along_axis(skewed, (m + t) & 7, axis=0)
    return pltpu.roll(picked, 0, 1, stride=EDGE, stride_axis=0)


def blocks_to_grid(half_rows, n):
    return jnp.concatenate(
        [
            jnp.concatenate(
                [turn_chunks(rows[8 * g : 8 * g + 8]) for g in range(n // 8)], axis=1
            )
            for rows in half_rows
        ],
        axis=0,
    )


def grid_to_blocks(plane, n):
    return [
        jnp.concatenate(
            [
                turn_chunks(plane[8 * h : 8 * h + 8, LANES * g : LANES * g + LANES])
                for g in range(n // 8)
            ],
            axis=0,
        )
        for h in range(2)
    ]


def shift_x(plane):
    width = plane.shape[1]
    return (pltpu.roll(plane, width - 1, 1), pltpu.roll(plane, 1, 1))


def shift_y(plane, low, high):
    y = iota(plane.shape, 0)
    return (
        jnp.where(y == EDGE - 1, high, pltpu.roll(plane, EDGE - 1, 0)),
        jnp.where(y == 0, low, pltpu.roll(plane, 1, 0)),
    )


def central(pair):
    return (pair[0] - pair[1]) * 0.5


def cross(a, b):
    return [
        a[1] * b[2] - a[2] * b[1],
        a[2] * b[0] - a[0] * b[2],
        a[0] * b[1] - a[1] * b[0],
    ]


def kernel(
    cols, rows, depth,
    vel, mag, table, fine, mag_new,
    field, own, ids_send, ids, v_send, v_got, w_got, f_send, f_got,
    by_send, by, bz, ey_send, ey, emf, ez,
    load_sems, send_sems, entered, ids_sem, v_sem, w_sem, f_sem, by_sem, bz_sems, ey_sem, ez_sems,
):
    n = cols * rows
    me, z = lax.axis_index("xy"), lax.axis_index("gz")
    first, last = z == 0, z == depth - 1

    def at_offset(j):
        return ((me // rows + j // rows) & (cols - 1)) * rows + ((me + j) & (rows - 1))

    def hops(j):
        return min(j // rows, cols - j // rows) + min(j % rows, rows - j % rows)

    def order_of(xy):
        y = xy & (rows - 1)
        return jnp.where(2 * y < rows, y, 3 * rows // 2 - 1 - y) * cols + xy // rows

    def rank(xy):
        return jnp.where(first, jnp.where(xy == 0, 1, 0), jnp.where(last, order_of(xy), 0))

    my_rank = rank(me)
    farthest_first = sorted(range(1, n), key=hops, reverse=True)
    peers = [(xy, rank(xy)) for xy in map(at_offset, farthest_first)]
    alike = jnp.where(first, n - 2 + my_rank, jnp.where(last, my_rank, n - 1))

    def each_ready(act):
        for xy, its_rank in peers:
            pl.when(its_rank <= my_rank)(functools.partial(act, xy))

    def each_later(act):
        for xy, its_rank in peers:
            pl.when(its_rank > my_rank)(functools.partial(act, xy))

    above, below = lax.rem(me + 1, n), lax.rem(me + n - 1, n)
    upper, lower = lax.rem(z + 1, depth), lax.rem(z + depth - 1, depth)

    loads = [
        pltpu.make_async_copy(table, own, load_sems.at[0]),
        *(pltpu.make_async_copy(vel.at[c], fine.at[c], load_sems.at[1 + c]) for c in range(3)),
        pltpu.make_async_copy(mag, field, load_sems.at[4]),
    ]

    barrier = pltpu.get_barrier_semaphore()

    def greet(xy, gz):
        pl.semaphore_signal(barrier, inc=1, device_id=(xy, gz), device_id_type=MESH)

    for xy, its_rank in peers:
        pl.when(its_rank >= my_rank)(functools.partial(greet, xy, z))

    @pl.when(jnp.logical_not(last))
    def _():
        greet(me, upper)

    @pl.when(first)
    def _():
        for xy in range(n):
            greet(xy, lower)

    loads[4].start()
    for load in loads[:4]:
        load.start()
    greetings = alike + jnp.where(first, 0, 1) + jnp.where(last, n, 0)

    @pl.when(greetings > 0)
    def _():
        pl.semaphore_wait(barrier, greetings)

    def say_entered(xy):
        pl.semaphore_signal(entered.at[me], inc=1, device_id=(xy, z), device_id_type=MESH)

    @pl.when(my_rank > 0)
    def _():
        for xy, its_rank in peers:
            pl.when(its_rank < my_rank)(functools.partial(say_entered, xy))

    def remote(src, dst, sent, got, xy, gz):
        return pltpu.make_async_remote_copy(
            src_ref=src, dst_ref=dst, send_sem=sent, recv_sem=got,
            device_id=(xy, gz), device_id_type=MESH,
        )

    up_xy = remote(
        mag.at[pl.ds(0, 2), 1], bz.at[0, pl.ds(0, 2)], send_sems.at[1], bz_sems.at[0], me, upper
    )
    up_z = remote(mag.at[2, 1], bz.at[0, 2], send_sems.at[13], bz_sems.at[2], me, upper)
    down = remote(mag.at[:, 0], bz.at[1], send_sems.at[2], bz_sems.at[1], me, lower)
    edges = [
        remote(by_send.at[0], by.at[0], send_sems.at[3], by_sem.at[0], above, z),
        remote(by_send.at[1], by.at[1], send_sems.at[4], by_sem.at[1], below, z),
    ]

    @pl.when(last)
    def _():
        up_xy.start()
        up_z.start()

    @pl.when(jnp.logical_not(first))
    def _():
        down.start()

    f_cell, c_cell = iota((1024, 256), 0), iota((1024, 256), 1)
    c_y = c_cell // LANES * 8 + (-(c_cell // EDGE) & 7)
    to_coarse = jnp.where(
        (f_cell // 64 == c_y) & (f_cell % 32 // 2 == c_cell % 16), 0.125, 0.0
    ).astype(jnp.bfloat16)
    loads[0].wait()
    own_row = own[...]
    ids_send[...] = jnp.full((1, LANES), -1, jnp.int32)
    ids_send[:, 0:n] = own_row
    ids[pl.ds(me, 1), :] = ids_send[...]

    def send_ids(xy):
        there = ids.at[pl.ds(me, 1)]
        remote(ids_send, there, send_sems.at[11], ids_sem, xy, z).start()

    each_ready(send_ids)

    pick = one_hot(own_row // n == iota((n, n), 0))
    pick = pick.astype(jnp.bfloat16)
    pick2 = jnp.concatenate([pick, pick], axis=1)

    for c in range(3):
        loads[1 + c].wait()
        pair = jnp.concatenate(
            [fine[c, 0] + fine[c, 1], fine[c, 2] + fine[c, 3]], axis=0
        )
        both = dot(stacked_halves(pair), to_coarse)
        mean = both[: 2 * n] + both[2 * n :]
        by_slot = jnp.concatenate([mean[:n], mean[n:]], axis=1)
        by_peer = dot(pick2, stacked_halves(by_slot))
        for k in range(2):
            for h in range(2):
                at = LANES * (2 * k + h)
                v_send[:, 6 * k + 2 * c + h, :] = by_peer[:, at : at + LANES]

    def send_v(xy):
        remote(v_send.at[xy], v_got.at[me], send_sems.at[12], v_sem, xy, z).start()

    upper_rows = pl.ds(6, 6)

    @pl.when(last)
    def _():
        for xy in range(n):
            remote(v_send.at[xy, upper_rows], w_got.at[me], send_sems.at[0], w_sem, xy, upper).start()

    each_ready(send_v)

    loads[4].wait()
    for p in range(6):
        by_send[0, p : p + 1, :] = field[p // 2, p % 2, EDGE - 1 : EDGE, :]
        by_send[1, p : p + 1, :] = field[p // 2, p % 2, 0:1, :]
    v_got[me] = v_send[me]

    @pl.when(jnp.logical_or(first, last))
    def _():
        @each_later
        def _(xy):
            pl.semaphore_wait(entered.at[xy], 1)
            send_ids(xy)
            send_v(xy)

    for edge in edges:
        edge.start()

    @pl.when(jnp.logical_not(last))
    def _():
        down.wait_recv()
        up_xy.start()
        up_z.start()

    def wait_all(ref, sem):
        rest = ref.at[pl.ds(0, n - 1)]
        pltpu.make_async_copy(rest, rest, sem).wait()

    wait_all(ids, ids_sem)
    listed = ids[...]
    column = jnp.where((listed >= 0) & (listed // n == me), lax.rem(listed, n), 0).astype(jnp.float32)
    of_peer = jnp.sum(column, axis=1, keepdims=True)
    lane = iota((n, n), 1)
    turned = lane // 8 * 8 + (-lane & 7)
    give = one_hot(of_peer == turned.astype(jnp.float32)).astype(jnp.bfloat16)
    give2 = jnp.concatenate([give, give], axis=1)
    column_row = lax.dot_general(
        jnp.ones((n, LANES), jnp.bfloat16), column.astype(jnp.bfloat16),
        (((1,), (1,)), ((), ())), preferred_element_type=jnp.float32,
    )
    take = one_hot(column_row == iota((n, n), 0).astype(jnp.float32)).astype(jnp.bfloat16)
    take2 = jnp.concatenate([take, take], axis=1)

    def on_grid(ref, planes):
        together = jnp.concatenate([ref[:, r, :] for r in range(6 * planes)], axis=1)
        blocks = dot(take2, stacked_halves(together))
        parts = [blocks[:, LANES * r : LANES * r + LANES] for r in range(6 * planes)]
        return [
            [blocks_to_grid(parts[6 * k + 2 * c : 6 * k + 2 * c + 2], n) for c in range(3)]
            for k in range(planes)
        ]

    up2 = remote(emf.at[1, pl.ds(0, 2)], ez.at[0], send_sems.at[7], ez_sems.at[0], me, upper)
    down2 = remote(emf.at[0, pl.ds(0, 2)], ez.at[1], send_sems.at[8], ez_sems.at[1], me, lower)
    edges2 = [
        remote(ey_send.at[0], ey.at[0], send_sems.at[9], ey_sem.at[0], above, z),
        remote(ey_send.at[1], ey.at[1], send_sems.at[10], ey_sem.at[1], below, z),
    ]

    def make_emf():
        wait_all(v_got, v_sem)
        flow = on_grid(v_got, 2)
        for k in range(2):
            e = cross(flow[k], [field[c, k] for c in range(3)])
            for c in range(3):
                emf[k, c] = e[c]
            for i, c in enumerate((0, 2)):
                ey_send[0, 2 * i + k : 2 * i + k + 1, :] = e[c][EDGE - 1 : EDGE, :]
                ey_send[1, 2 * i + k : 2 * i + k + 1, :] = e[c][0:1, :]

        @pl.when(jnp.logical_not(last))
        def _():
            up2.start()

        for edge in edges2:
            edge.start()

    @pl.when(first)
    def _():
        make_emf()

    for edge in edges:
        edge.wait_recv()

    @pl.when(last)
    def _():
        down.wait_recv()

    def make_force(k):
        b = [field[c, k] for c in range(3)]
        along_x = [shift_x(b[c]) for c in range(3)]
        along_y = [
            shift_y(b[c], by[0, 2 * c + k : 2 * c + k + 1, :], by[1, 2 * c + k : 2 * c + k + 1, :])
            for c in range(3)
        ]

        def along_z(c):
            return (bz[1, c], field[c, 0]) if k else (field[c, 1], bz[0, c])

        dx, dy = ([central(pair) for pair in pairs] for pairs in (along_x, along_y))
        dz = [central(along_z(c)) for c in range(2)]
        current = [dy[2] - dz[1], dz[0] - dx[2], dx[1] - dy[0]]
        tiles = [tile for f in cross(current, b) for tile in grid_to_blocks(0.1 * f, n)]
        by_peer = dot(give2, stacked_halves(jnp.concatenate(tiles, axis=1)))
        for r in range(HALF_ROWS):
            f_send[k, :, r, :] = by_peer[:, LANES * r : LANES * r + LANES]
        for xy, _ in peers:
            remote(f_send.at[k, xy], f_got.at[k, me], send_sems.at[5 + k], f_sem.at[k], xy, z).start()
        f_got[k, me] = f_send[k, me]
        if not k:
            up_z.wait_recv()
        for c in range(3):
            z_pair = along_z(c)
            lap = (
                (z_pair[0] + z_pair[1])
                + (along_y[c][0] + along_y[c][1])
                + (along_x[c][0] + along_x[c][1])
                - 6.0 * b[c]
            )
            mag_new[c, k] = b[c] + 0.05 * lap

    make_force(1)
    up_xy.wait_recv()

    @pl.when(first)
    def _():
        down.start()

    make_force(0)

    @pl.when(jnp.logical_not(first))
    def _():
        make_emf()

    down2.start()

    s_sub, s_lane = iota((n, n), 0), iota((n, n), 1)
    own_diagonal = jnp.where(s_sub == s_lane, own_row // n, 0).astype(jnp.float32).astype(jnp.bfloat16)
    row_of_slot = lax.dot_general(
        own_diagonal, jnp.ones((n, n), jnp.bfloat16),
        (((1,), (1,)), ((), ())), preferred_element_type=jnp.float32,
    )
    back = one_hot(row_of_slot == s_lane.astype(jnp.float32)).astype(jnp.bfloat16)
    c_cell2, f_cell2 = iota((256, 1024), 0), iota((256, 1024), 1)
    to_fine = one_hot(
        (f_cell2 // 64 == c_cell2 // 16) & (f_cell2 % 32 // 2 == c_cell2 % 16)
    ).astype(jnp.bfloat16)

    def update(k):
        wait_all(f_got.at[k], f_sem.at[k])
        high, low = halves(jnp.concatenate([f_got[k, :, r, :] for r in range(HALF_ROWS)], axis=1))
        parts = [dot(back, part).astype(jnp.bfloat16) for part in (high, low)]
        wide = dot(
            jnp.concatenate([part[:, 256 * c : 256 * c + 256] for part in parts for c in range(3)], axis=0),
            to_fine,
        )
        for c in range(3):
            gain = wide[n * c : n * c + n] + wide[n * (3 + c) : n * (4 + c)]
            fine[c, 2 * k] += gain
            fine[c, 2 * k + 1] += gain

    def finish():
        @pl.when(jnp.logical_not(first))
        def _():
            up2.wait_recv()

        @pl.when(first)
        def _():
            every = w_got.at[:]
            pltpu.make_async_copy(every, every, w_sem).wait()
            [below_flow] = on_grid(w_got, 1)
            e = cross(below_flow, [bz[0, c] for c in range(3)])
            for c in range(2):
                ez[0, c] = e[c]

        down2.wait_recv()
        for edge in edges2:
            edge.wait_recv()

        def dz(c, k):
            return central((emf[1, c], ez[0, c]) if k == 0 else (ez[1, c], emf[0, c]))

        def dy(c, k):
            i = 2 * (c // 2) + k
            return central(shift_y(emf[k, c], ey[0, i : i + 1, :], ey[1, i : i + 1, :]))

        def dx(c, k):
            return central(shift_x(emf[k, c]))

        for k in range(2):
            mag_new[0, k] += 0.1 * (dy(2, k) - dz(1, k))
            mag_new[1, k] += 0.1 * (dz(0, k) - dx(2, k))
            mag_new[2, k] += 0.1 * (dx(1, k) - dy(0, k))

    update(1)
    finish()
    update(0)

    for edge in [up_xy, up_z, down, down2, *edges, *edges2]:
        edge.wait_send()

    @pl.when(jnp.logical_not(last))
    def _():
        up2.wait_send()

    @pl.when(last)
    def _():
        every = w_got.at[:]
        pltpu.make_async_copy(every, every, send_sems.at[0]).wait()

    wait_all(ids, send_sems.at[11])
    wait_all(v_send, send_sems.at[12])
    for k in range(2):
        wait_all(f_send.at[k], send_sems.at[5 + k])


def write_out(fine, mag_new, vel_out, mag_out, sems):
    copies = [
        pltpu.make_async_copy(fine.at[c, pl.ds(2 * k, 2)], vel_out.at[c, pl.ds(2 * k, 2)], sems.at[2 * c + k])
        for c in range(3)
        for k in range(2)
    ]
    copies += [pltpu.make_async_copy(mag_new, mag_out, sems.at[6])]
    for copy in copies:
        copy.start()
    for copy in copies:
        copy.wait()


def body(cols, rows, depth, velocity, magnetic, slot_block_table):
    n = cols * rows
    width = EDGE * n
    f32 = jnp.float32
    far = pl.BlockSpec(memory_space=pl.ANY)
    near = pl.BlockSpec(memory_space=pltpu.VMEM)
    dma = pltpu.SemaphoreType.DMA
    fine, mag_new = pl.pallas_call(
        functools.partial(kernel, cols, rows, depth),
        out_shape=(
            pltpu.VMEM(velocity.shape, f32),
            pltpu.VMEM(magnetic.shape, f32),
        ),
        in_specs=[far, far, far],
        out_specs=(near, near),
        scratch_shapes=[
            pltpu.VMEM((3, 2, EDGE, width), f32),
            pltpu.VMEM((1, n), jnp.int32),
            pltpu.VMEM((1, LANES), jnp.int32),
            pltpu.VMEM((n, LANES), jnp.int32),
            pltpu.VMEM((n, ROWS, LANES), f32),
            pltpu.VMEM((n, ROWS, LANES), f32),
            pltpu.VMEM((n, 6, LANES), f32),
            pltpu.VMEM((2, n, HALF_ROWS, LANES), f32),
            pltpu.VMEM((2, n, HALF_ROWS, LANES), f32),
            pltpu.VMEM((2, 6, width), f32),
            pltpu.VMEM((2, 6, width), f32),
            pltpu.VMEM((2, 3, EDGE, width), f32),
            pltpu.VMEM((2, 4, width), f32),
            pltpu.VMEM((2, 4, width), f32),
            pltpu.VMEM((2, 3, EDGE, width), f32),
            pltpu.VMEM((2, 2, EDGE, width), f32),
            dma((5,)), dma((14,)), pltpu.SemaphoreType.REGULAR((n,)), dma, dma, dma, dma((2,)), dma((2,)), dma((3,)), dma((2,)), dma((2,)),
        ],
        compiler_params=pltpu.CompilerParams(
            collective_id=0, has_side_effects=True, vmem_limit_bytes=60 << 20
        ),
        name="dynamo_substep",
    )(velocity, magnetic, slot_block_table.reshape(1, n))
    return pl.pallas_call(
        write_out,
        out_shape=(
            jax.ShapeDtypeStruct(velocity.shape, f32),
            jax.ShapeDtypeStruct(magnetic.shape, f32),
        ),
        in_specs=[near, near],
        out_specs=(far, far),
        scratch_shapes=[dma((7,))],
        name="write_out",
    )(*(pltpu.with_memory_space_constraint(a, pltpu.VMEM) for a in (fine, mag_new)))


def solution(mesh):
    n, depth = mesh.shape["xy"], mesh.shape["gz"]
    rows = {32: 8, 8: 4}[n]
    spec = P(None, "gz", "xy", None)
    return jax.shard_map(
        functools.partial(body, n // rows, rows, depth),
        mesh=mesh,
        in_specs=(spec, spec, P("xy")),
        out_specs=(spec, spec),
        check_vma=False,
    )
```

```python
import functools

import jax
import jax.numpy as jnp
from jax import lax
from jax.experimental import pallas as pl
from jax.experimental.pallas import tpu as pltpu
from jax.sharding import PartitionSpec as P

MESH = pl.DeviceIdType.MESH
LANES = 128
EDGE = 16
ROWS = 12
HALF_ROWS = 6


def halves(value):
    high = value.astype(jnp.bfloat16)
    return high, (value - high.astype(jnp.float32)).astype(jnp.bfloat16)


def stacked_halves(value):
    return jnp.concatenate(halves(value), axis=0)


def dot(a, b):
    return jnp.dot(a, b, preferred_element_type=jnp.float32)


def iota(shape, dim):
    return lax.broadcasted_iota(jnp.int32, shape, dim)


def one_hot(condition):
    return jnp.where(condition, 1.0, 0.0)


def turn_chunks(tile):
    t, m = iota((8, LANES), 0), iota((8, LANES), 1) // EDGE
    skewed = pltpu.roll(tile, 0, 1, stride=EDGE, stride_axis=0)
    picked = jnp.take_along_axis(skewed, (m + t) & 7, axis=0)
    return pltpu.roll(picked, 0, 1, stride=EDGE, stride_axis=0)


def blocks_to_grid(half_rows, n):
    return jnp.concatenate(
        [
            jnp.concatenate(
                [turn_chunks(rows[8 * g : 8 * g + 8]) for g in range(n // 8)], axis=1
            )
            for rows in half_rows
        ],
        axis=0,
    )


def grid_to_blocks(plane, n):
    return [
        jnp.concatenate(
            [
                turn_chunks(plane[8 * h : 8 * h + 8, LANES * g : LANES * g + LANES])
                for g in range(n // 8)
            ],
            axis=0,
        )
        for h in range(2)
    ]


def shift_x(plane):
    width = plane.shape[1]
    return (pltpu.roll(plane, width - 1, 1), pltpu.roll(plane, 1, 1))


def shift_y(plane, low, high):
    y = iota(plane.shape, 0)
    return (
        jnp.where(y == EDGE - 1, high, pltpu.roll(plane, EDGE - 1, 0)),
        jnp.where(y == 0, low, pltpu.roll(plane, 1, 0)),
    )


def central(pair):
    return (pair[0] - pair[1]) * 0.5


def cross(a, b):
    return [
        a[1] * b[2] - a[2] * b[1],
        a[2] * b[0] - a[0] * b[2],
        a[0] * b[1] - a[1] * b[0],
    ]


def kernel(
    cols, rows, depth,
    vel, mag, table, fine, mag_new,
    field, own, ids_send, ids, v_send, v_got, w_got, f_send, f_got,
    by_send, by, bz, ey_send, ey, emf, ez,
    load_sems, send_sems, entered, ids_sem, v_sem, w_sem, f_sem, by_sem, bz_sems, ey_sem, ez_sems,
):
    n = cols * rows
    me, z = lax.axis_index("xy"), lax.axis_index("gz")
    first, last = z == 0, z == depth - 1

    def at_offset(j):
        return ((me // rows + j // rows) & (cols - 1)) * rows + ((me + j) & (rows - 1))

    def hops(j):
        return min(j // rows, cols - j // rows) + min(j % rows, rows - j % rows)

    def order_of(xy):
        y = xy & (rows - 1)
        return jnp.where(2 * y < rows, y, 3 * rows // 2 - 1 - y) * cols + xy // rows

    def rank(xy):
        return jnp.where(first, jnp.where(xy == 0, 1, 0), jnp.where(last, order_of(xy), 0))

    my_rank = rank(me)
    farthest_first = sorted(range(1, n), key=hops, reverse=True)
    peers = [(xy, rank(xy)) for xy in map(at_offset, farthest_first)]
    alike = jnp.where(first, n - 2 + my_rank, jnp.where(last, my_rank, n - 1))

    def each_ready(act):
        for xy, its_rank in peers:
            pl.when(its_rank <= my_rank)(functools.partial(act, xy))

    def each_later(act):
        for xy, its_rank in peers:
            pl.when(its_rank > my_rank)(functools.partial(act, xy))

    above, below = lax.rem(me + 1, n), lax.rem(me + n - 1, n)
    upper, lower = lax.rem(z + 1, depth), lax.rem(z + depth - 1, depth)

    loads = [
        pltpu.make_async_copy(table, own, load_sems.at[0]),
        *(pltpu.make_async_copy(vel.at[c], fine.at[c], load_sems.at[1 + c]) for c in range(3)),
        pltpu.make_async_copy(mag, field, load_sems.at[4]),
    ]

    barrier = pltpu.get_barrier_semaphore()

    def greet(xy, gz):
        pl.semaphore_signal(barrier, inc=1, device_id=(xy, gz), device_id_type=MESH)

    @pl.when(last)
    def _():
        places = [x * rows + y for y in (*range(rows // 2), *range(rows - 1, rows // 2 - 1, -1)) for x in range(cols)]
        for q in range(1, n):
            pl.when(q > my_rank)(functools.partial(greet, places[q], z))

    @pl.when(jnp.logical_not(jnp.logical_or(last, my_rank > 0)))
    def _():
        for j in farthest_first:
            greet(at_offset(j), z)

    @pl.when(jnp.logical_not(last))
    def _():
        greet(me, upper)

    @pl.when(first)
    def _():
        for xy in range(n):
            greet(xy, lower)

    loads[4].start()
    for load in loads[:4]:
        load.start()
    f_cell, c_cell = iota((1024, 256), 0), iota((1024, 256), 1)
    c_y = c_cell // LANES * 8 + (-(c_cell // EDGE) & 7)
    to_coarse = jnp.where(
        (f_cell // 64 == c_y) & (f_cell % 32 // 2 == c_cell % 16), 0.125, 0.0
    ).astype(jnp.bfloat16)
    greetings = alike + jnp.where(first, 0, 1) + jnp.where(last, n, 0)

    @pl.when(greetings > 0)
    def _():
        pl.semaphore_wait(barrier, greetings)

    def remote(src, dst, sent, got, xy, gz):
        return pltpu.make_async_remote_copy(
            src_ref=src, dst_ref=dst, send_sem=sent, recv_sem=got,
            device_id=(xy, gz), device_id_type=MESH,
        )

    up_xy = remote(
        mag.at[pl.ds(0, 2), 1], bz.at[0, pl.ds(0, 2)], send_sems.at[1], bz_sems.at[0], me, upper
    )
    up_z = remote(mag.at[2, 1], bz.at[0, 2], send_sems.at[13], bz_sems.at[2], me, upper)
    down = remote(mag.at[:, 0], bz.at[1], send_sems.at[2], bz_sems.at[1], me, lower)
    edges = [
        remote(by_send.at[0], by.at[0], send_sems.at[3], by_sem.at[0], above, z),
        remote(by_send.at[1], by.at[1], send_sems.at[4], by_sem.at[1], below, z),
    ]

    @pl.when(last)
    def _():
        up_xy.start()
        up_z.start()

    def say_entered(xy):
        pl.semaphore_signal(entered.at[me], inc=1, device_id=(xy, z), device_id_type=MESH)

    @pl.when(my_rank > 0)
    def _():
        for xy, its_rank in peers:
            pl.when(its_rank < my_rank)(functools.partial(say_entered, xy))

    @pl.when(jnp.logical_not(first))
    def _():
        down.start()

    loads[0].wait()
    own_row = own[...]
    ids_send[...] = jnp.full((1, LANES), -1, jnp.int32)
    ids_send[:, 0:n] = own_row
    ids[pl.ds(me, 1), :] = ids_send[...]

    def send_ids(xy):
        there = ids.at[pl.ds(me, 1)]
        remote(ids_send, there, send_sems.at[11], ids_sem, xy, z).start()

    each_ready(send_ids)

    pick = one_hot(own_row // n == iota((n, n), 0))
    pick = pick.astype(jnp.bfloat16)
    pick2 = jnp.concatenate([pick, pick], axis=1)

    for c in range(3):
        loads[1 + c].wait()
        pair = jnp.concatenate(
            [fine[c, 0] + fine[c, 1], fine[c, 2] + fine[c, 3]], axis=0
        )
        both = dot(stacked_halves(pair), to_coarse)
        mean = both[: 2 * n] + both[2 * n :]
        by_slot = jnp.concatenate([mean[:n], mean[n:]], axis=1)
        by_peer = dot(pick2, stacked_halves(by_slot))
        for k in range(2):
            for h in range(2):
                at = LANES * (2 * k + h)
                v_send[:, 6 * k + 2 * c + h, :] = by_peer[:, at : at + LANES]

    def send_v(xy):
        remote(v_send.at[xy], v_got.at[me], send_sems.at[12], v_sem, xy, z).start()

    upper_rows = pl.ds(6, 6)

    @pl.when(last)
    def _():
        for xy in range(n):
            remote(v_send.at[xy, upper_rows], w_got.at[me], send_sems.at[0], w_sem, xy, upper).start()

    each_ready(send_v)

    loads[4].wait()
    for p in range(6):
        by_send[0, p : p + 1, :] = field[p // 2, p % 2, EDGE - 1 : EDGE, :]
        by_send[1, p : p + 1, :] = field[p // 2, p % 2, 0:1, :]
    v_got[me] = v_send[me]

    @pl.when(jnp.logical_or(first, last))
    def _():
        @each_later
        def _(xy):
            pl.semaphore_wait(entered.at[xy], 1)
            send_ids(xy)
            send_v(xy)

    for edge in edges:
        edge.start()

    @pl.when(jnp.logical_not(last))
    def _():
        down.wait_recv()
        up_xy.start()
        up_z.start()

    def wait_all(ref, sem):
        rest = ref.at[pl.ds(0, n - 1)]
        pltpu.make_async_copy(rest, rest, sem).wait()

    wait_all(ids, ids_sem)
    listed = ids[...]
    column = jnp.where((listed >= 0) & (listed // n == me), lax.rem(listed, n), 0).astype(jnp.float32)
    of_peer = jnp.sum(column, axis=1, keepdims=True)
    lane = iota((n, n), 1)
    turned = lane // 8 * 8 + (-lane & 7)
    give = one_hot(of_peer == turned.astype(jnp.float32)).astype(jnp.bfloat16)
    give2 = jnp.concatenate([give, give], axis=1)
    column_row = lax.dot_general(
        jnp.ones((n, LANES), jnp.bfloat16), column.astype(jnp.bfloat16),
        (((1,), (1,)), ((), ())), preferred_element_type=jnp.float32,
    )
    take = one_hot(column_row == iota((n, n), 0).astype(jnp.float32)).astype(jnp.bfloat16)
    take2 = jnp.concatenate([take, take], axis=1)

    def on_grid(ref, planes):
        together = jnp.concatenate([ref[:, r, :] for r in range(6 * planes)], axis=1)
        blocks = dot(take2, stacked_halves(together))
        parts = [blocks[:, LANES * r : LANES * r + LANES] for r in range(6 * planes)]
        return [
            [blocks_to_grid(parts[6 * k + 2 * c : 6 * k + 2 * c + 2], n) for c in range(3)]
            for k in range(planes)
        ]

    up2 = remote(emf.at[1, pl.ds(0, 2)], ez.at[0], send_sems.at[7], ez_sems.at[0], me, upper)
    down2 = remote(emf.at[0, pl.ds(0, 2)], ez.at[1], send_sems.at[8], ez_sems.at[1], me, lower)
    edges2 = [
        remote(ey_send.at[0], ey.at[0], send_sems.at[9], ey_sem.at[0], above, z),
        remote(ey_send.at[1], ey.at[1], send_sems.at[10], ey_sem.at[1], below, z),
    ]

    def make_emf():
        wait_all(v_got, v_sem)
        flow = on_grid(v_got, 2)
        for k in range(2):
            e = cross(flow[k], [field[c, k] for c in range(3)])
            for c in range(3):
                emf[k, c] = e[c]
            for i, c in enumerate((0, 2)):
                ey_send[0, 2 * i + k : 2 * i + k + 1, :] = e[c][EDGE - 1 : EDGE, :]
                ey_send[1, 2 * i + k : 2 * i + k + 1, :] = e[c][0:1, :]

        @pl.when(jnp.logical_not(last))
        def _():
            up2.start()

        for edge in edges2:
            edge.start()

    @pl.when(first)
    def _():
        make_emf()

    for edge in edges:
        edge.wait_recv()

    @pl.when(last)
    def _():
        down.wait_recv()

    def across(k):
        b = [field[c, k] for c in range(3)]
        along_x = [shift_x(b[c]) for c in range(3)]
        along_y = [
            shift_y(b[c], by[0, 2 * c + k : 2 * c + k + 1, :], by[1, 2 * c + k : 2 * c + k + 1, :])
            for c in range(3)
        ]
        return b, along_x, along_y

    def make_force(k, b, along_x, along_y):
        def along_z(c):
            return (bz[1, c], field[c, 0]) if k else (field[c, 1], bz[0, c])

        dx, dy = ([central(pair) for pair in pairs] for pairs in (along_x, along_y))
        dz = [central(along_z(c)) for c in range(2)]
        current = [dy[2] - dz[1], dz[0] - dx[2], dx[1] - dy[0]]
        tiles = [tile for f in cross(current, b) for tile in grid_to_blocks(0.1 * f, n)]
        by_peer = dot(give2, stacked_halves(jnp.concatenate(tiles, axis=1)))
        for r in range(HALF_ROWS):
            f_send[k, :, r, :] = by_peer[:, LANES * r : LANES * r + LANES]
        for xy, _ in peers:
            remote(f_send.at[k, xy], f_got.at[k, me], send_sems.at[5 + k], f_sem.at[k], xy, z).start()
        f_got[k, me] = f_send[k, me]
        if not k:
            up_z.wait_recv()
        for c in range(3):
            z_pair = along_z(c)
            lap = (
                (z_pair[0] + z_pair[1])
                + (along_y[c][0] + along_y[c][1])
                + (along_x[c][0] + along_x[c][1])
                - 6.0 * b[c]
            )
            mag_new[c, k] = b[c] + 0.05 * lap

    make_force(1, *across(1))
    prepared = across(0)
    up_xy.wait_recv()

    @pl.when(first)
    def _():
        down.start()

    make_force(0, *prepared)

    @pl.when(jnp.logical_not(first))
    def _():
        make_emf()

    down2.start()

    s_sub, s_lane = iota((n, n), 0), iota((n, n), 1)
    own_diagonal = jnp.where(s_sub == s_lane, own_row // n, 0).astype(jnp.float32).astype(jnp.bfloat16)
    row_of_slot = lax.dot_general(
        own_diagonal, jnp.ones((n, n), jnp.bfloat16),
        (((1,), (1,)), ((), ())), preferred_element_type=jnp.float32,
    )
    back = one_hot(row_of_slot == s_lane.astype(jnp.float32)).astype(jnp.bfloat16)
    c_cell2, f_cell2 = iota((256, 1024), 0), iota((256, 1024), 1)
    to_fine = one_hot(
        (f_cell2 // 64 == c_cell2 // 16) & (f_cell2 % 32 // 2 == c_cell2 % 16)
    ).astype(jnp.bfloat16)

    def update(k):
        wait_all(f_got.at[k], f_sem.at[k])
        high, low = halves(jnp.concatenate([f_got[k, :, r, :] for r in range(HALF_ROWS)], axis=1))
        parts = [dot(back, part).astype(jnp.bfloat16) for part in (high, low)]
        wide = dot(
            jnp.concatenate([part[:, 256 * c : 256 * c + 256] for part in parts for c in range(3)], axis=0),
            to_fine,
        )
        for c in range(3):
            gain = wide[n * c : n * c + n] + wide[n * (3 + c) : n * (4 + c)]
            fine[c, 2 * k] += gain
            fine[c, 2 * k + 1] += gain

    def finish():
        down2.wait_recv()
        for edge in edges2:
            edge.wait_recv()

        def dz(c, k):
            return (emf[1, c] if k == 0 else ez[1, c] - emf[0, c]) * 0.5

        def dy(c, k):
            i = 2 * (c // 2) + k
            return central(shift_y(emf[k, c], ey[0, i : i + 1, :], ey[1, i : i + 1, :]))

        def dx(c, k):
            return central(shift_x(emf[k, c]))

        for k in range(2):
            mag_new[0, k] += 0.1 * (dy(2, k) - dz(1, k))
            mag_new[1, k] += 0.1 * (dz(0, k) - dx(2, k))
            mag_new[2, k] += 0.1 * (dx(1, k) - dy(0, k))

    def finish_below():
        @pl.when(jnp.logical_not(first))
        def _():
            up2.wait_recv()

        @pl.when(first)
        def _():
            every = w_got.at[:]
            pltpu.make_async_copy(every, every, w_sem).wait()
            [below_flow] = on_grid(w_got, 1)
            e = cross(below_flow, [bz[0, c] for c in range(3)])
            for c in range(2):
                ez[0, c] = e[c]

        mag_new[0, 0] += 0.05 * ez[0, 1]
        mag_new[1, 0] -= 0.05 * ez[0, 0]

    update(1)
    finish()
    finish_below()
    update(0)

    for edge in [up_xy, up_z, down, down2, *edges, *edges2]:
        edge.wait_send()

    @pl.when(jnp.logical_not(last))
    def _():
        up2.wait_send()

    @pl.when(last)
    def _():
        every = w_got.at[:]
        pltpu.make_async_copy(every, every, send_sems.at[0]).wait()

    wait_all(ids, send_sems.at[11])
    wait_all(v_send, send_sems.at[12])
    for k in range(2):
        wait_all(f_send.at[k], send_sems.at[5 + k])


def write_out(fine, mag_new, vel_out, mag_out, sems):
    copies = [
        pltpu.make_async_copy(fine.at[c, pl.ds(2 * k, 2)], vel_out.at[c, pl.ds(2 * k, 2)], sems.at[2 * c + k])
        for c in range(3)
        for k in range(2)
    ]
    copies += [pltpu.make_async_copy(mag_new, mag_out, sems.at[6])]
    for copy in copies:
        copy.start()
    for copy in copies:
        copy.wait()


def body(cols, rows, depth, velocity, magnetic, slot_block_table):
    n = cols * rows
    width = EDGE * n
    f32 = jnp.float32
    far = pl.BlockSpec(memory_space=pl.ANY)
    near = pl.BlockSpec(memory_space=pltpu.VMEM)
    dma = pltpu.SemaphoreType.DMA
    fine, mag_new = pl.pallas_call(
        functools.partial(kernel, cols, rows, depth),
        out_shape=(
            pltpu.VMEM(velocity.shape, f32),
            pltpu.VMEM(magnetic.shape, f32),
        ),
        in_specs=[far, far, far],
        out_specs=(near, near),
        scratch_shapes=[
            pltpu.VMEM((3, 2, EDGE, width), f32),
            pltpu.VMEM((1, n), jnp.int32),
            pltpu.VMEM((1, LANES), jnp.int32),
            pltpu.VMEM((n, LANES), jnp.int32),
            pltpu.VMEM((n, ROWS, LANES), f32),
            pltpu.VMEM((n, ROWS, LANES), f32),
            pltpu.VMEM((n, 6, LANES), f32),
            pltpu.VMEM((2, n, HALF_ROWS, LANES), f32),
            pltpu.VMEM((2, n, HALF_ROWS, LANES), f32),
            pltpu.VMEM((2, 6, width), f32),
            pltpu.VMEM((2, 6, width), f32),
            pltpu.VMEM((2, 3, EDGE, width), f32),
            pltpu.VMEM((2, 4, width), f32),
            pltpu.VMEM((2, 4, width), f32),
            pltpu.VMEM((2, 3, EDGE, width), f32),
            pltpu.VMEM((2, 2, EDGE, width), f32),
            dma((5,)), dma((14,)), pltpu.SemaphoreType.REGULAR((n,)), dma, dma, dma, dma((2,)), dma((2,)), dma((3,)), dma((2,)), dma((2,)),
        ],
        compiler_params=pltpu.CompilerParams(
            collective_id=0, has_side_effects=True, vmem_limit_bytes=60 << 20
        ),
        name="dynamo_substep",
    )(velocity, magnetic, slot_block_table.reshape(1, n))
    return pl.pallas_call(
        write_out,
        out_shape=(
            jax.ShapeDtypeStruct(velocity.shape, f32),
            jax.ShapeDtypeStruct(magnetic.shape, f32),
        ),
        in_specs=[near, near],
        out_specs=(far, far),
        scratch_shapes=[dma((7,))],
        name="write_out",
    )(*(pltpu.with_memory_space_constraint(a, pltpu.VMEM) for a in (fine, mag_new)))


def solution(mesh):
    n, depth = mesh.shape["xy"], mesh.shape["gz"]
    rows = {32: 8, 8: 4}[n]
    spec = P(None, "gz", "xy", None)
    return jax.shard_map(
        functools.partial(body, n // rows, rows, depth),
        mesh=mesh,
        in_specs=(spec, spec, P("xy")),
        out_specs=(spec, spec),
        check_vma=False,
    )
```

```python
import functools

import jax
import jax.numpy as jnp
from jax import lax
from jax.experimental import pallas as pl
from jax.experimental.pallas import tpu as pltpu
from jax.sharding import PartitionSpec as P

MESH = pl.DeviceIdType.MESH
LANES = 128
EDGE = 16
ROWS = 12
HALF_ROWS = 6


def halves(value):
    high = value.astype(jnp.bfloat16)
    return high, (value - high.astype(jnp.float32)).astype(jnp.bfloat16)


def stacked_halves(value):
    return jnp.concatenate(halves(value), axis=0)


def dot(a, b):
    return jnp.dot(a, b, preferred_element_type=jnp.float32)


def iota(shape, dim):
    return lax.broadcasted_iota(jnp.int32, shape, dim)


def one_hot(condition):
    return jnp.where(condition, 1.0, 0.0)


def turn_chunks(tile):
    t, m = iota((8, LANES), 0), iota((8, LANES), 1) // EDGE
    skewed = pltpu.roll(tile, 0, 1, stride=EDGE, stride_axis=0)
    picked = jnp.take_along_axis(skewed, (m + t) & 7, axis=0)
    return pltpu.roll(picked, 0, 1, stride=EDGE, stride_axis=0)


def blocks_to_grid(half_rows, n):
    return jnp.concatenate(
        [
            jnp.concatenate(
                [turn_chunks(rows[8 * g : 8 * g + 8]) for g in range(n // 8)], axis=1
            )
            for rows in half_rows
        ],
        axis=0,
    )


def grid_to_blocks(plane, n):
    return [
        jnp.concatenate(
            [
                turn_chunks(plane[8 * h : 8 * h + 8, LANES * g : LANES * g + LANES])
                for g in range(n // 8)
            ],
            axis=0,
        )
        for h in range(2)
    ]


def shift_x(plane):
    width = plane.shape[1]
    return (pltpu.roll(plane, width - 1, 1), pltpu.roll(plane, 1, 1))


def shift_y(plane, low, high):
    y = iota(plane.shape, 0)
    return (
        jnp.where(y == EDGE - 1, high, pltpu.roll(plane, EDGE - 1, 0)),
        jnp.where(y == 0, low, pltpu.roll(plane, 1, 0)),
    )


def central(pair):
    return (pair[0] - pair[1]) * 0.5


def cross(a, b):
    return [
        a[1] * b[2] - a[2] * b[1],
        a[2] * b[0] - a[0] * b[2],
        a[0] * b[1] - a[1] * b[0],
    ]


def gains(blocks, back, to_fine):
    n = back.shape[0]
    high, low = halves(jnp.concatenate([blocks[:, r, :] for r in range(HALF_ROWS)], axis=1))
    parts = [dot(back, part).astype(jnp.bfloat16) for part in (high, low)]
    wide = dot(
        jnp.concatenate([part[:, 256 * c : 256 * c + 256] for part in parts for c in range(3)], axis=0),
        to_fine,
    )
    return [wide[n * c : n * c + n] + wide[n * (3 + c) : n * (4 + c)] for c in range(3)]


def kernel(
    cols, rows, depth,
    vel, mag, table, fine, mag_new, f_got, back_out, to_fine_out,
    field, own, ids_send, ids, v_send, v_got, w_got, f_send, f_got_1,
    by_send, by, bz, ey_send, ey, emf, ez,
    load_sems, send_sems, entered, ids_sem, v_sem, w_sem, f_sem, by_sem, bz_sems, ey_sem, ez_sems,
):
    n = cols * rows
    me, z = lax.axis_index("xy"), lax.axis_index("gz")
    first, last = z == 0, z == depth - 1

    def at_offset(j):
        return ((me // rows + j // rows) & (cols - 1)) * rows + ((me + j) & (rows - 1))

    def hops(j):
        return min(j // rows, cols - j // rows) + min(j % rows, rows - j % rows)

    def order_of(xy):
        y = xy & (rows - 1)
        return jnp.where(2 * y < rows, y, 3 * rows // 2 - 1 - y) * cols + xy // rows

    def rank(xy):
        return jnp.where(first, jnp.where(xy == 0, 1, 0), jnp.where(last, order_of(xy), 0))

    my_rank = rank(me)
    farthest_first = sorted(range(1, n), key=hops, reverse=True)
    peers = [(xy, rank(xy)) for xy in map(at_offset, farthest_first)]
    alike = jnp.where(first, n - 2 + my_rank, jnp.where(last, my_rank, n - 1))

    def each_ready(act):
        for xy, its_rank in peers:
            pl.when(its_rank <= my_rank)(functools.partial(act, xy))

    def each_later(act):
        for xy, its_rank in peers:
            pl.when(its_rank > my_rank)(functools.partial(act, xy))

    above, below = lax.rem(me + 1, n), lax.rem(me + n - 1, n)
    upper, lower = lax.rem(z + 1, depth), lax.rem(z + depth - 1, depth)

    loads = [
        pltpu.make_async_copy(table, own, load_sems.at[0]),
        *(pltpu.make_async_copy(vel.at[c], fine.at[c], load_sems.at[1 + c]) for c in range(3)),
        pltpu.make_async_copy(mag, field, load_sems.at[4]),
    ]

    barrier = pltpu.get_barrier_semaphore()

    def greet(xy, gz):
        pl.semaphore_signal(barrier, inc=1, device_id=(xy, gz), device_id_type=MESH)

    @pl.when(last)
    def _():
        places = [x * rows + y for y in (*range(rows // 2), *range(rows - 1, rows // 2 - 1, -1)) for x in range(cols)]
        for q in range(1, n):
            pl.when(q > my_rank)(functools.partial(greet, places[q], z))

    @pl.when(jnp.logical_not(jnp.logical_or(last, my_rank > 0)))
    def _():
        for j in farthest_first:
            greet(at_offset(j), z)

    @pl.when(jnp.logical_not(last))
    def _():
        greet(me, upper)

    @pl.when(first)
    def _():
        for xy in range(n):
            greet(xy, lower)

    loads[4].start()
    for load in loads[:4]:
        load.start()
    f_cell, c_cell = iota((1024, 256), 0), iota((1024, 256), 1)
    c_y = c_cell // LANES * 8 + (-(c_cell // EDGE) & 7)
    to_coarse = jnp.where(
        (f_cell // 64 == c_y) & (f_cell % 32 // 2 == c_cell % 16), 0.125, 0.0
    ).astype(jnp.bfloat16)
    greetings = alike + jnp.where(first, 0, 1) + jnp.where(last, n, 0)

    @pl.when(greetings > 0)
    def _():
        pl.semaphore_wait(barrier, greetings)

    def remote(src, dst, sent, got, xy, gz):
        return pltpu.make_async_remote_copy(
            src_ref=src, dst_ref=dst, send_sem=sent, recv_sem=got,
            device_id=(xy, gz), device_id_type=MESH,
        )

    up_xy = remote(
        mag.at[pl.ds(0, 2), 1], bz.at[0, pl.ds(0, 2)], send_sems.at[1], bz_sems.at[0], me, upper
    )
    up_z = remote(mag.at[2, 1], bz.at[0, 2], send_sems.at[13], bz_sems.at[2], me, upper)
    down = remote(mag.at[:, 0], bz.at[1], send_sems.at[2], bz_sems.at[1], me, lower)
    edges = [
        remote(by_send.at[0], by.at[0], send_sems.at[3], by_sem.at[0], above, z),
        remote(by_send.at[1], by.at[1], send_sems.at[4], by_sem.at[1], below, z),
    ]

    @pl.when(last)
    def _():
        up_xy.start()
        up_z.start()

    def say_entered(xy):
        pl.semaphore_signal(entered.at[me], inc=1, device_id=(xy, z), device_id_type=MESH)

    @pl.when(my_rank > 0)
    def _():
        for xy, its_rank in peers:
            pl.when(its_rank < my_rank)(functools.partial(say_entered, xy))

    @pl.when(jnp.logical_not(first))
    def _():
        down.start()

    loads[0].wait()
    own_row = own[...]
    ids_send[...] = jnp.full((1, LANES), -1, jnp.int32)
    ids_send[:, 0:n] = own_row
    ids[pl.ds(me, 1), :] = ids_send[...]

    def send_ids(xy):
        there = ids.at[pl.ds(me, 1)]
        remote(ids_send, there, send_sems.at[11], ids_sem, xy, z).start()

    each_ready(send_ids)

    pick = one_hot(own_row // n == iota((n, n), 0))
    pick = pick.astype(jnp.bfloat16)
    pick2 = jnp.concatenate([pick, pick], axis=1)

    for c in range(3):
        loads[1 + c].wait()
        pair = jnp.concatenate(
            [fine[c, 0] + fine[c, 1], fine[c, 2] + fine[c, 3]], axis=0
        )
        both = dot(stacked_halves(pair), to_coarse)
        mean = both[: 2 * n] + both[2 * n :]
        by_slot = jnp.concatenate([mean[:n], mean[n:]], axis=1)
        by_peer = dot(pick2, stacked_halves(by_slot))
        for k in range(2):
            for h in range(2):
                at = LANES * (2 * k + h)
                v_send[:, 6 * k + 2 * c + h, :] = by_peer[:, at : at + LANES]

    def send_v(xy):
        remote(v_send.at[xy], v_got.at[me], send_sems.at[12], v_sem, xy, z).start()

    upper_rows = pl.ds(6, 6)

    @pl.when(last)
    def _():
        for xy in range(n):
            remote(v_send.at[xy, upper_rows], w_got.at[me], send_sems.at[0], w_sem, xy, upper).start()

    each_ready(send_v)

    loads[4].wait()
    for p in range(6):
        by_send[0, p : p + 1, :] = field[p // 2, p % 2, EDGE - 1 : EDGE, :]
        by_send[1, p : p + 1, :] = field[p // 2, p % 2, 0:1, :]
    v_got[me] = v_send[me]

    @pl.when(jnp.logical_or(first, last))
    def _():
        @each_later
        def _(xy):
            pl.semaphore_wait(entered.at[xy], 1)
            send_ids(xy)
            send_v(xy)

    for edge in edges:
        edge.start()

    @pl.when(jnp.logical_not(last))
    def _():
        down.wait_recv()
        up_xy.start()
        up_z.start()

    def wait_all(ref, sem):
        rest = ref.at[pl.ds(0, n - 1)]
        pltpu.make_async_copy(rest, rest, sem).wait()

    wait_all(ids, ids_sem)
    listed = ids[...]
    column = jnp.where((listed >= 0) & (listed // n == me), lax.rem(listed, n), 0).astype(jnp.float32)
    of_peer = jnp.sum(column, axis=1, keepdims=True)
    lane = iota((n, n), 1)
    turned = lane // 8 * 8 + (-lane & 7)
    give = one_hot(of_peer == turned.astype(jnp.float32)).astype(jnp.bfloat16)
    give2 = jnp.concatenate([give, give], axis=1)
    column_row = lax.dot_general(
        jnp.ones((n, LANES), jnp.bfloat16), column.astype(jnp.bfloat16),
        (((1,), (1,)), ((), ())), preferred_element_type=jnp.float32,
    )
    take = one_hot(column_row == iota((n, n), 0).astype(jnp.float32)).astype(jnp.bfloat16)
    take2 = jnp.concatenate([take, take], axis=1)

    def on_grid(ref, planes):
        together = jnp.concatenate([ref[:, r, :] for r in range(6 * planes)], axis=1)
        blocks = dot(take2, stacked_halves(together))
        parts = [blocks[:, LANES * r : LANES * r + LANES] for r in range(6 * planes)]
        return [
            [blocks_to_grid(parts[6 * k + 2 * c : 6 * k + 2 * c + 2], n) for c in range(3)]
            for k in range(planes)
        ]

    up2 = remote(emf.at[1, pl.ds(0, 2)], ez.at[0], send_sems.at[7], ez_sems.at[0], me, upper)
    down2 = remote(emf.at[0, pl.ds(0, 2)], ez.at[1], send_sems.at[8], ez_sems.at[1], me, lower)
    edges2 = [
        remote(ey_send.at[0], ey.at[0], send_sems.at[9], ey_sem.at[0], above, z),
        remote(ey_send.at[1], ey.at[1], send_sems.at[10], ey_sem.at[1], below, z),
    ]

    def make_emf():
        wait_all(v_got, v_sem)
        flow = on_grid(v_got, 2)
        for k in range(2):
            e = cross(flow[k], [field[c, k] for c in range(3)])
            for c in range(3):
                emf[k, c] = e[c]
            for i, c in enumerate((0, 2)):
                ey_send[0, 2 * i + k : 2 * i + k + 1, :] = e[c][EDGE - 1 : EDGE, :]
                ey_send[1, 2 * i + k : 2 * i + k + 1, :] = e[c][0:1, :]

        @pl.when(jnp.logical_not(last))
        def _():
            up2.start()

        for edge in edges2:
            edge.start()

    @pl.when(first)
    def _():
        make_emf()

    for edge in edges:
        edge.wait_recv()

    @pl.when(last)
    def _():
        down.wait_recv()

    got = (f_got, f_got_1)

    def across(k):
        b = [field[c, k] for c in range(3)]
        along_x = [shift_x(b[c]) for c in range(3)]
        along_y = [
            shift_y(b[c], by[0, 2 * c + k : 2 * c + k + 1, :], by[1, 2 * c + k : 2 * c + k + 1, :])
            for c in range(3)
        ]
        return b, along_x, along_y

    def make_force(k, b, along_x, along_y):
        def along_z(c):
            return (bz[1, c], field[c, 0]) if k else (field[c, 1], bz[0, c])

        dx, dy = ([central(pair) for pair in pairs] for pairs in (along_x, along_y))
        dz = [central(along_z(c)) for c in range(2)]
        current = [dy[2] - dz[1], dz[0] - dx[2], dx[1] - dy[0]]
        tiles = [tile for f in cross(current, b) for tile in grid_to_blocks(0.1 * f, n)]
        by_peer = dot(give2, stacked_halves(jnp.concatenate(tiles, axis=1)))
        for r in range(HALF_ROWS):
            f_send[k, :, r, :] = by_peer[:, LANES * r : LANES * r + LANES]
        for xy, _ in peers:
            remote(f_send.at[k, xy], got[k].at[me], send_sems.at[5 + k], f_sem.at[k], xy, z).start()
        got[k][me] = f_send[k, me]
        if not k:
            up_z.wait_recv()
        for c in range(3):
            z_pair = along_z(c)
            lap = (
                (z_pair[0] + z_pair[1])
                + (along_y[c][0] + along_y[c][1])
                + (along_x[c][0] + along_x[c][1])
                - 6.0 * b[c]
            )
            mag_new[c, k] = b[c] + 0.05 * lap

    make_force(1, *across(1))
    prepared = across(0)
    up_xy.wait_recv()

    @pl.when(first)
    def _():
        down.start()

    make_force(0, *prepared)

    @pl.when(jnp.logical_not(first))
    def _():
        make_emf()

    down2.start()

    s_sub, s_lane = iota((n, n), 0), iota((n, n), 1)
    own_diagonal = jnp.where(s_sub == s_lane, own_row // n, 0).astype(jnp.float32).astype(jnp.bfloat16)
    row_of_slot = lax.dot_general(
        own_diagonal, jnp.ones((n, n), jnp.bfloat16),
        (((1,), (1,)), ((), ())), preferred_element_type=jnp.float32,
    )
    back = one_hot(row_of_slot == s_lane.astype(jnp.float32)).astype(jnp.bfloat16)
    c_cell2, f_cell2 = iota((256, 1024), 0), iota((256, 1024), 1)
    to_fine = one_hot(
        (f_cell2 // 64 == c_cell2 // 16) & (f_cell2 % 32 // 2 == c_cell2 % 16)
    ).astype(jnp.bfloat16)

    back_out[...] = back.astype(jnp.float32)
    to_fine_out[...] = to_fine

    def update_upper():
        wait_all(f_got_1, f_sem.at[1])
        for c, gain in enumerate(gains(f_got_1, back, to_fine)):
            fine[c, 2] += gain
            fine[c, 3] += gain

    def finish():
        down2.wait_recv()
        for edge in edges2:
            edge.wait_recv()

        def dz(c, k):
            return (emf[1, c] if k == 0 else ez[1, c] - emf[0, c]) * 0.5

        def dy(c, k):
            i = 2 * (c // 2) + k
            return central(shift_y(emf[k, c], ey[0, i : i + 1, :], ey[1, i : i + 1, :]))

        def dx(c, k):
            return central(shift_x(emf[k, c]))

        for k in range(2):
            mag_new[0, k] += 0.1 * (dy(2, k) - dz(1, k))
            mag_new[1, k] += 0.1 * (dz(0, k) - dx(2, k))
            mag_new[2, k] += 0.1 * (dx(1, k) - dy(0, k))

    def finish_below():
        @pl.when(jnp.logical_not(first))
        def _():
            up2.wait_recv()

        @pl.when(first)
        def _():
            every = w_got.at[:]
            pltpu.make_async_copy(every, every, w_sem).wait()
            [below_flow] = on_grid(w_got, 1)
            e = cross(below_flow, [bz[0, c] for c in range(3)])
            for c in range(2):
                ez[0, c] = e[c]

        mag_new[0, 0] += 0.05 * ez[0, 1]
        mag_new[1, 0] -= 0.05 * ez[0, 0]

    update_upper()
    finish()
    finish_below()
    wait_all(f_got, f_sem.at[0])

    for edge in [up_xy, up_z, down, down2, *edges, *edges2]:
        edge.wait_send()

    @pl.when(jnp.logical_not(last))
    def _():
        up2.wait_send()

    @pl.when(last)
    def _():
        every = w_got.at[:]
        pltpu.make_async_copy(every, every, send_sems.at[0]).wait()

    wait_all(ids, send_sems.at[11])
    wait_all(v_send, send_sems.at[12])
    for k in range(2):
        wait_all(f_send.at[k], send_sems.at[5 + k])


def write_out(fine, mag_new, f_got, back, to_fine, vel_out, mag_out, lower, sems):
    def written(k, c, ref):
        return pltpu.make_async_copy(ref, vel_out.at[c, pl.ds(2 * k, 2)], sems.at[3 * k + c])

    copies = [written(1, c, fine.at[c, pl.ds(2, 2)]) for c in range(3)]
    copies += [pltpu.make_async_copy(mag_new, mag_out, sems.at[6])]
    for copy in copies:
        copy.start()
    for c, gain in enumerate(gains(f_got, back[...].astype(jnp.bfloat16), to_fine[...])):
        lower[c, 0] = fine[c, 0] + gain
        lower[c, 1] = fine[c, 1] + gain
        copies.append(written(0, c, lower.at[c]))
        copies[-1].start()
    for copy in copies:
        copy.wait()


def body(cols, rows, depth, velocity, magnetic, slot_block_table):
    n = cols * rows
    width = EDGE * n
    f32 = jnp.float32
    far = pl.BlockSpec(memory_space=pl.ANY)
    near = pl.BlockSpec(memory_space=pltpu.VMEM)
    dma = pltpu.SemaphoreType.DMA
    made = pl.pallas_call(
        functools.partial(kernel, cols, rows, depth),
        out_shape=(
            pltpu.VMEM(velocity.shape, f32),
            pltpu.VMEM(magnetic.shape, f32),
            pltpu.VMEM((n, HALF_ROWS, LANES), f32),
            pltpu.VMEM((n, n), f32),
            pltpu.VMEM((256, 1024), jnp.bfloat16),
        ),
        in_specs=[far, far, far],
        out_specs=(near,) * 5,
        scratch_shapes=[
            pltpu.VMEM((3, 2, EDGE, width), f32),
            pltpu.VMEM((1, n), jnp.int32),
            pltpu.VMEM((1, LANES), jnp.int32),
            pltpu.VMEM((n, LANES), jnp.int32),
            pltpu.VMEM((n, ROWS, LANES), f32),
            pltpu.VMEM((n, ROWS, LANES), f32),
            pltpu.VMEM((n, 6, LANES), f32),
            pltpu.VMEM((2, n, HALF_ROWS, LANES), f32),
            pltpu.VMEM((n, HALF_ROWS, LANES), f32),
            pltpu.VMEM((2, 6, width), f32),
            pltpu.VMEM((2, 6, width), f32),
            pltpu.VMEM((2, 3, EDGE, width), f32),
            pltpu.VMEM((2, 4, width), f32),
            pltpu.VMEM((2, 4, width), f32),
            pltpu.VMEM((2, 3, EDGE, width), f32),
            pltpu.VMEM((2, 2, EDGE, width), f32),
            dma((5,)), dma((14,)), pltpu.SemaphoreType.REGULAR((n,)), dma, dma, dma, dma((2,)), dma((2,)), dma((3,)), dma((2,)), dma((2,)),
        ],
        compiler_params=pltpu.CompilerParams(
            collective_id=0, has_side_effects=True, vmem_limit_bytes=60 << 20
        ),
        name="dynamo_substep",
    )(velocity, magnetic, slot_block_table.reshape(1, n))
    return pl.pallas_call(
        write_out,
        out_shape=(
            jax.ShapeDtypeStruct(velocity.shape, f32),
            jax.ShapeDtypeStruct(magnetic.shape, f32),
        ),
        in_specs=[near] * 5,
        out_specs=(far, far),
        scratch_shapes=[pltpu.VMEM((3, 2, n, 1024), f32), dma((7,))],
        compiler_params=pltpu.CompilerParams(vmem_limit_bytes=16 << 20),
        name="write_out",
    )(*(pltpu.with_memory_space_constraint(a, pltpu.VMEM) for a in made))


def solution(mesh):
    n, depth = mesh.shape["xy"], mesh.shape["gz"]
    rows = {32: 8, 8: 4}[n]
    spec = P(None, "gz", "xy", None)
    return jax.shard_map(
        functools.partial(body, n // rows, rows, depth),
        mesh=mesh,
        in_specs=(spec, spec, P("xy")),
        out_specs=(spec, spec),
        check_vma=False,
    )
```

```python
import functools

import jax
import jax.numpy as jnp
from jax import lax
from jax.experimental import pallas as pl
from jax.experimental.pallas import tpu as pltpu
from jax.sharding import PartitionSpec as P

MESH = pl.DeviceIdType.MESH
LANES = 128
EDGE = 16
ROWS = 12
HALF_ROWS = 6


def halves(value):
    high = value.astype(jnp.bfloat16)
    return high, (value - high.astype(jnp.float32)).astype(jnp.bfloat16)


def stacked_halves(value):
    return jnp.concatenate(halves(value), axis=0)


def dot(a, b):
    return jnp.dot(a, b, preferred_element_type=jnp.float32)


def iota(shape, dim):
    return lax.broadcasted_iota(jnp.int32, shape, dim)


def one_hot(condition):
    return jnp.where(condition, 1.0, 0.0)


def turn_chunks(tile):
    t, m = iota((8, LANES), 0), iota((8, LANES), 1) // EDGE
    skewed = pltpu.roll(tile, 0, 1, stride=EDGE, stride_axis=0)
    picked = jnp.take_along_axis(skewed, (m + t) & 7, axis=0)
    return pltpu.roll(picked, 0, 1, stride=EDGE, stride_axis=0)


def blocks_to_grid(half_rows, n):
    return jnp.concatenate(
        [
            jnp.concatenate(
                [turn_chunks(rows[8 * g : 8 * g + 8]) for g in range(n // 8)], axis=1
            )
            for rows in half_rows
        ],
        axis=0,
    )


def grid_to_blocks(plane, n):
    return [
        jnp.concatenate(
            [
                turn_chunks(plane[8 * h : 8 * h + 8, LANES * g : LANES * g + LANES])
                for g in range(n // 8)
            ],
            axis=0,
        )
        for h in range(2)
    ]


def shift_x(plane):
    width = plane.shape[1]
    return (pltpu.roll(plane, width - 1, 1), pltpu.roll(plane, 1, 1))


def shift_y(plane, low, high):
    y = iota(plane.shape, 0)
    return (
        jnp.where(y == EDGE - 1, high, pltpu.roll(plane, EDGE - 1, 0)),
        jnp.where(y == 0, low, pltpu.roll(plane, 1, 0)),
    )


def central(pair):
    return (pair[0] - pair[1]) * 0.5


def cross(a, b):
    return [
        a[1] * b[2] - a[2] * b[1],
        a[2] * b[0] - a[0] * b[2],
        a[0] * b[1] - a[1] * b[0],
    ]


def gains(blocks, back, to_fine):
    n = back.shape[0]
    high, low = halves(jnp.concatenate([blocks[:, r, :] for r in range(HALF_ROWS)], axis=1))
    parts = [dot(back, part).astype(jnp.bfloat16) for part in (high, low)]
    wide = dot(
        jnp.concatenate([part[:, 256 * c : 256 * c + 256] for part in parts for c in range(3)], axis=0),
        to_fine,
    )
    return [wide[n * c : n * c + n] + wide[n * (3 + c) : n * (4 + c)] for c in range(3)]


def kernel(
    cols, rows, depth,
    vel, mag, table, fine, mag_new, f_got, back_out, to_fine_out,
    field, own, ids_send, ids, v_send, v_got, w_got, f_send, f_got_1,
    by_send, by, bz, ey_send, ey, emf, ez,
    load_sems, send_sems, entered, ids_sem, v_sem, w_sem, f_sem, by_sem, bz_sems, ey_sem, ez_sems,
):
    n = cols * rows
    me, z = lax.axis_index("xy"), lax.axis_index("gz")
    first, last = z == 0, z == depth - 1

    def at_offset(j):
        return ((me // rows + j // rows) & (cols - 1)) * rows + ((me + j) & (rows - 1))

    def hops(j):
        return min(j // rows, cols - j // rows) + min(j % rows, rows - j % rows)

    def order_of(xy):
        y = xy & (rows - 1)
        return jnp.where(2 * y < rows, y, 3 * rows // 2 - 1 - y) * cols + xy // rows

    def rank(xy):
        return jnp.where(first, jnp.where(xy == 0, 1, 0), jnp.where(last, order_of(xy), 0))

    my_rank = rank(me)
    farthest_first = sorted(range(1, n), key=hops, reverse=True)
    peers = [(xy, rank(xy)) for xy in map(at_offset, farthest_first)]
    alike = jnp.where(first, n - 2 + my_rank, jnp.where(last, my_rank, n - 1))

    def each_ready(act):
        for xy, its_rank in peers:
            pl.when(its_rank <= my_rank)(functools.partial(act, xy))

    def each_later(act):
        for xy, its_rank in peers:
            pl.when(its_rank > my_rank)(functools.partial(act, xy))

    above, below = lax.rem(me + 1, n), lax.rem(me + n - 1, n)
    upper, lower = lax.rem(z + 1, depth), lax.rem(z + depth - 1, depth)

    loads = [
        pltpu.make_async_copy(table, own, load_sems.at[0]),
        *(pltpu.make_async_copy(vel.at[c], fine.at[c], load_sems.at[1 + c]) for c in range(3)),
        pltpu.make_async_copy(mag, field, load_sems.at[4]),
    ]

    barrier = pltpu.get_barrier_semaphore()

    def greet(xy, gz):
        pl.semaphore_signal(barrier, inc=1, device_id=(xy, gz), device_id_type=MESH)

    @pl.when(last)
    def _():
        places = [x * rows + y for y in (*range(rows // 2), *range(rows - 1, rows // 2 - 1, -1)) for x in range(cols)]
        for q in range(n - 1, 0, -1):
            pl.when(q > my_rank)(functools.partial(greet, places[q], z))

    @pl.when(jnp.logical_not(jnp.logical_or(last, my_rank > 0)))
    def _():
        for j in farthest_first:
            greet(at_offset(j), z)

    @pl.when(jnp.logical_not(last))
    def _():
        greet(me, upper)

    @pl.when(first)
    def _():
        for xy in range(n):
            greet(xy, lower)

    loads[4].start()
    for load in loads[:4]:
        load.start()
    f_cell, c_cell = iota((1024, 256), 0), iota((1024, 256), 1)
    c_y = c_cell // LANES * 8 + (-(c_cell // EDGE) & 7)
    to_coarse = jnp.where(
        (f_cell // 64 == c_y) & (f_cell % 32 // 2 == c_cell % 16), 0.125, 0.0
    ).astype(jnp.bfloat16)
    greetings = alike + jnp.where(first, 0, 1) + jnp.where(last, n, 0)

    @pl.when(greetings > 0)
    def _():
        pl.semaphore_wait(barrier, greetings)

    def remote(src, dst, sent, got, xy, gz):
        return pltpu.make_async_remote_copy(
            src_ref=src, dst_ref=dst, send_sem=sent, recv_sem=got,
            device_id=(xy, gz), device_id_type=MESH,
        )

    up_xy = remote(
        mag.at[pl.ds(0, 2), 1], bz.at[0, pl.ds(0, 2)], send_sems.at[1], bz_sems.at[0], me, upper
    )
    up_z = remote(mag.at[2, 1], bz.at[0, 2], send_sems.at[13], bz_sems.at[2], me, upper)
    down = remote(mag.at[:, 0], bz.at[1], send_sems.at[2], bz_sems.at[1], me, lower)
    edges = [
        remote(by_send.at[0], by.at[0], send_sems.at[3], by_sem.at[0], above, z),
        remote(by_send.at[1], by.at[1], send_sems.at[4], by_sem.at[1], below, z),
    ]

    @pl.when(last)
    def _():
        up_xy.start()
        up_z.start()

    def say_entered(xy):
        pl.semaphore_signal(entered.at[me], inc=1, device_id=(xy, z), device_id_type=MESH)

    @pl.when(my_rank > 0)
    def _():
        for xy, its_rank in peers:
            pl.when(its_rank < my_rank)(functools.partial(say_entered, xy))

    @pl.when(jnp.logical_not(first))
    def _():
        down.start()

    loads[0].wait()
    own_row = own[...]
    ids_send[...] = jnp.full((1, LANES), -1, jnp.int32)
    ids_send[:, 0:n] = own_row
    ids[pl.ds(me, 1), :] = ids_send[...]

    def send_ids(xy):
        there = ids.at[pl.ds(me, 1)]
        remote(ids_send, there, send_sems.at[11], ids_sem, xy, z).start()

    each_ready(send_ids)

    pick = one_hot(own_row // n == iota((n, n), 0))
    pick = pick.astype(jnp.bfloat16)
    pick2 = jnp.concatenate([pick, pick], axis=1)

    for c in range(3):
        loads[1 + c].wait()
        pair = jnp.concatenate(
            [fine[c, 0] + fine[c, 1], fine[c, 2] + fine[c, 3]], axis=0
        )
        both = dot(stacked_halves(pair), to_coarse)
        mean = both[: 2 * n] + both[2 * n :]
        by_slot = jnp.concatenate([mean[:n], mean[n:]], axis=1)
        by_peer = dot(pick2, stacked_halves(by_slot))
        for k in range(2):
            for h in range(2):
                at = LANES * (2 * k + h)
                v_send[:, 6 * k + 2 * c + h, :] = by_peer[:, at : at + LANES]

    def send_v(xy):
        remote(v_send.at[xy], v_got.at[me], send_sems.at[12], v_sem, xy, z).start()

    upper_rows = pl.ds(6, 6)

    @pl.when(last)
    def _():
        for xy in range(n):
            remote(v_send.at[xy, upper_rows], w_got.at[me], send_sems.at[0], w_sem, xy, upper).start()

    each_ready(send_v)

    loads[4].wait()
    for p in range(6):
        by_send[0, p : p + 1, :] = field[p // 2, p % 2, EDGE - 1 : EDGE, :]
        by_send[1, p : p + 1, :] = field[p // 2, p % 2, 0:1, :]
    v_got[me] = v_send[me]

    @pl.when(jnp.logical_or(first, last))
    def _():
        @each_later
        def _(xy):
            pl.semaphore_wait(entered.at[xy], 1)
            send_ids(xy)
            send_v(xy)

    for edge in edges:
        edge.start()

    @pl.when(jnp.logical_not(last))
    def _():
        down.wait_recv()
        up_xy.start()
        up_z.start()

    def wait_all(ref, sem):
        rest = ref.at[pl.ds(0, n - 1)]
        pltpu.make_async_copy(rest, rest, sem).wait()

    wait_all(ids, ids_sem)
    listed = ids[...]
    column = jnp.where((listed >= 0) & (listed // n == me), lax.rem(listed, n), 0).astype(jnp.float32)
    of_peer = jnp.sum(column, axis=1, keepdims=True)
    lane = iota((n, n), 1)
    turned = lane // 8 * 8 + (-lane & 7)
    give = one_hot(of_peer == turned.astype(jnp.float32)).astype(jnp.bfloat16)
    give2 = jnp.concatenate([give, give], axis=1)
    column_row = lax.dot_general(
        jnp.ones((n, LANES), jnp.bfloat16), column.astype(jnp.bfloat16),
        (((1,), (1,)), ((), ())), preferred_element_type=jnp.float32,
    )
    take = one_hot(column_row == iota((n, n), 0).astype(jnp.float32)).astype(jnp.bfloat16)
    take2 = jnp.concatenate([take, take], axis=1)

    def on_grid(ref, planes):
        together = jnp.concatenate([ref[:, r, :] for r in range(6 * planes)], axis=1)
        blocks = dot(take2, stacked_halves(together))
        parts = [blocks[:, LANES * r : LANES * r + LANES] for r in range(6 * planes)]
        return [
            [blocks_to_grid(parts[6 * k + 2 * c : 6 * k + 2 * c + 2], n) for c in range(3)]
            for k in range(planes)
        ]

    up2 = remote(emf.at[1, pl.ds(0, 2)], ez.at[0], send_sems.at[7], ez_sems.at[0], me, upper)
    down2 = remote(emf.at[0, pl.ds(0, 2)], ez.at[1], send_sems.at[8], ez_sems.at[1], me, lower)
    edges2 = [
        remote(ey_send.at[0], ey.at[0], send_sems.at[9], ey_sem.at[0], above, z),
        remote(ey_send.at[1], ey.at[1], send_sems.at[10], ey_sem.at[1], below, z),
    ]

    def make_emf():
        wait_all(v_got, v_sem)
        flow = on_grid(v_got, 2)
        for k in range(2):
            e = cross(flow[k], [field[c, k] for c in range(3)])
            for c in range(3):
                emf[k, c] = e[c]
            for i, c in enumerate((0, 2)):
                ey_send[0, 2 * i + k : 2 * i + k + 1, :] = e[c][EDGE - 1 : EDGE, :]
                ey_send[1, 2 * i + k : 2 * i + k + 1, :] = e[c][0:1, :]

        @pl.when(jnp.logical_not(last))
        def _():
            up2.start()

        for edge in edges2:
            edge.start()

    @pl.when(first)
    def _():
        make_emf()

    for edge in edges:
        edge.wait_recv()

    @pl.when(last)
    def _():
        down.wait_recv()

    got = (f_got, f_got_1)

    def across(k):
        b = [field[c, k] for c in range(3)]
        along_x = [shift_x(b[c]) for c in range(3)]
        along_y = [
            shift_y(b[c], by[0, 2 * c + k : 2 * c + k + 1, :], by[1, 2 * c + k : 2 * c + k + 1, :])
            for c in range(3)
        ]
        return b, along_x, along_y

    def make_force(k, b, along_x, along_y):
        def along_z(c):
            return (bz[1, c], field[c, 0]) if k else (field[c, 1], bz[0, c])

        dx, dy = ([central(pair) for pair in pairs] for pairs in (along_x, along_y))
        dz = [central(along_z(c)) for c in range(2)]
        current = [dy[2] - dz[1], dz[0] - dx[2], dx[1] - dy[0]]
        tiles = [tile for f in cross(current, b) for tile in grid_to_blocks(0.1 * f, n)]
        by_peer = dot(give2, stacked_halves(jnp.concatenate(tiles, axis=1)))
        for r in range(HALF_ROWS):
            f_send[k, :, r, :] = by_peer[:, LANES * r : LANES * r + LANES]
        for xy, _ in peers:
            remote(f_send.at[k, xy], got[k].at[me], send_sems.at[5 + k], f_sem.at[k], xy, z).start()
        got[k][me] = f_send[k, me]
        if not k:
            up_z.wait_recv()
        for c in range(3):
            z_pair = along_z(c)
            lap = (
                (z_pair[0] + z_pair[1])
                + (along_y[c][0] + along_y[c][1])
                + (along_x[c][0] + along_x[c][1])
                - 6.0 * b[c]
            )
            mag_new[c, k] = b[c] + 0.05 * lap

    make_force(1, *across(1))
    prepared = across(0)
    up_xy.wait_recv()

    @pl.when(first)
    def _():
        down.start()

    make_force(0, *prepared)

    @pl.when(jnp.logical_not(first))
    def _():
        make_emf()

    down2.start()

    s_sub, s_lane = iota((n, n), 0), iota((n, n), 1)
    own_diagonal = jnp.where(s_sub == s_lane, own_row // n, 0).astype(jnp.float32).astype(jnp.bfloat16)
    row_of_slot = lax.dot_general(
        own_diagonal, jnp.ones((n, n), jnp.bfloat16),
        (((1,), (1,)), ((), ())), preferred_element_type=jnp.float32,
    )
    back = one_hot(row_of_slot == s_lane.astype(jnp.float32)).astype(jnp.bfloat16)
    c_cell2, f_cell2 = iota((256, 1024), 0), iota((256, 1024), 1)
    to_fine = one_hot(
        (f_cell2 // 64 == c_cell2 // 16) & (f_cell2 % 32 // 2 == c_cell2 % 16)
    ).astype(jnp.bfloat16)

    back_out[...] = back.astype(jnp.float32)
    to_fine_out[...] = to_fine

    def update_upper():
        wait_all(f_got_1, f_sem.at[1])
        for c, gain in enumerate(gains(f_got_1, back, to_fine)):
            fine[c, 2] += gain
            fine[c, 3] += gain

    def finish():
        down2.wait_recv()
        for edge in edges2:
            edge.wait_recv()

        def dz(c, k):
            return (emf[1, c] if k == 0 else ez[1, c] - emf[0, c]) * 0.5

        def dy(c, k):
            i = 2 * (c // 2) + k
            return central(shift_y(emf[k, c], ey[0, i : i + 1, :], ey[1, i : i + 1, :]))

        def dx(c, k):
            return central(shift_x(emf[k, c]))

        for k in range(2):
            mag_new[0, k] += 0.1 * (dy(2, k) - dz(1, k))
            mag_new[1, k] += 0.1 * (dz(0, k) - dx(2, k))
            mag_new[2, k] += 0.1 * (dx(1, k) - dy(0, k))

    def finish_below():
        @pl.when(jnp.logical_not(first))
        def _():
            up2.wait_recv()

        @pl.when(first)
        def _():
            every = w_got.at[:]
            pltpu.make_async_copy(every, every, w_sem).wait()
            [below_flow] = on_grid(w_got, 1)
            e = cross(below_flow, [bz[0, c] for c in range(3)])
            for c in range(2):
                ez[0, c] = e[c]

        mag_new[0, 0] += 0.05 * ez[0, 1]
        mag_new[1, 0] -= 0.05 * ez[0, 0]

    update_upper()
    finish()
    finish_below()
    wait_all(f_got, f_sem.at[0])

    for edge in [up_xy, up_z, down, down2, *edges, *edges2]:
        edge.wait_send()

    @pl.when(jnp.logical_not(last))
    def _():
        up2.wait_send()

    @pl.when(last)
    def _():
        every = w_got.at[:]
        pltpu.make_async_copy(every, every, send_sems.at[0]).wait()

    wait_all(ids, send_sems.at[11])
    wait_all(v_send, send_sems.at[12])
    for k in range(2):
        wait_all(f_send.at[k], send_sems.at[5 + k])


def write_out(fine, mag_new, f_got, back, to_fine, vel_out, mag_out, lower, sems):
    def written(k, c, ref):
        return pltpu.make_async_copy(ref, vel_out.at[c, pl.ds(2 * k, 2)], sems.at[3 * k + c])

    copies = [written(1, c, fine.at[c, pl.ds(2, 2)]) for c in range(3)]
    copies += [pltpu.make_async_copy(mag_new, mag_out, sems.at[6])]
    for copy in copies:
        copy.start()
    for c, gain in enumerate(gains(f_got, back[...].astype(jnp.bfloat16), to_fine[...])):
        lower[c, 0] = fine[c, 0] + gain
        lower[c, 1] = fine[c, 1] + gain
        copies.append(written(0, c, lower.at[c]))
        copies[-1].start()
    for copy in copies:
        copy.wait()


def body(cols, rows, depth, velocity, magnetic, slot_block_table):
    n = cols * rows
    width = EDGE * n
    f32 = jnp.float32
    far = pl.BlockSpec(memory_space=pl.ANY)
    near = pl.BlockSpec(memory_space=pltpu.VMEM)
    dma = pltpu.SemaphoreType.DMA
    made = pl.pallas_call(
        functools.partial(kernel, cols, rows, depth),
        out_shape=(
            pltpu.VMEM(velocity.shape, f32),
            pltpu.VMEM(magnetic.shape, f32),
            pltpu.VMEM((n, HALF_ROWS, LANES), f32),
            pltpu.VMEM((n, n), f32),
            pltpu.VMEM((256, 1024), jnp.bfloat16),
        ),
        in_specs=[far, far, far],
        out_specs=(near,) * 5,
        scratch_shapes=[
            pltpu.VMEM((3, 2, EDGE, width), f32),
            pltpu.VMEM((1, n), jnp.int32),
            pltpu.VMEM((1, LANES), jnp.int32),
            pltpu.VMEM((n, LANES), jnp.int32),
            pltpu.VMEM((n, ROWS, LANES), f32),
            pltpu.VMEM((n, ROWS, LANES), f32),
            pltpu.VMEM((n, 6, LANES), f32),
            pltpu.VMEM((2, n, HALF_ROWS, LANES), f32),
            pltpu.VMEM((n, HALF_ROWS, LANES), f32),
            pltpu.VMEM((2, 6, width), f32),
            pltpu.VMEM((2, 6, width), f32),
            pltpu.VMEM((2, 3, EDGE, width), f32),
            pltpu.VMEM((2, 4, width), f32),
            pltpu.VMEM((2, 4, width), f32),
            pltpu.VMEM((2, 3, EDGE, width), f32),
            pltpu.VMEM((2, 2, EDGE, width), f32),
            dma((5,)), dma((14,)), pltpu.SemaphoreType.REGULAR((n,)), dma, dma, dma, dma((2,)), dma((2,)), dma((3,)), dma((2,)), dma((2,)),
        ],
        compiler_params=pltpu.CompilerParams(
            collective_id=0, has_side_effects=True, vmem_limit_bytes=60 << 20
        ),
        name="dynamo_substep",
    )(velocity, magnetic, slot_block_table.reshape(1, n))
    return pl.pallas_call(
        write_out,
        out_shape=(
            jax.ShapeDtypeStruct(velocity.shape, f32),
            jax.ShapeDtypeStruct(magnetic.shape, f32),
        ),
        in_specs=[near] * 5,
        out_specs=(far, far),
        scratch_shapes=[pltpu.VMEM((3, 2, n, 1024), f32), dma((7,))],
        compiler_params=pltpu.CompilerParams(vmem_limit_bytes=16 << 20),
        name="write_out",
    )(*(pltpu.with_memory_space_constraint(a, pltpu.VMEM) for a in made))


def solution(mesh):
    n, depth = mesh.shape["xy"], mesh.shape["gz"]
    rows = {32: 8, 8: 4}[n]
    spec = P(None, "gz", "xy", None)
    return jax.shard_map(
        functools.partial(body, n // rows, rows, depth),
        mesh=mesh,
        in_specs=(spec, spec, P("xy")),
        out_specs=(spec, spec),
        check_vma=False,
    )
```
